256 devices in a mesh: prow: 16 (over z, core), pcol: 16 (over x, y).
Axes of the slice: x: 4, y: 4, z: 8, core: 2. Of those that a mesh axis runs over, the one named last changes fastest.
Arguments:
- leaf_source: bfloat16 [16, 16, 8, 256, 128], P('prow', 'pcol'), may hold values from -6 to 6
- band_source: bfloat16 [16, 256, 128], P('prow'), may hold values from -6 to 6
- strip_source: bfloat16 [16, 256, 128], P('pcol'), may hold values from -6 to 6
- summit_source: bfloat16 [256, 128], replicated, may hold values from -6 to 6
- leaf_inverse: bfloat16 [16, 16, 8, 256, 256], P('prow', 'pcol'), may hold values from -1 to 2
- band_inverse: bfloat16 [16, 256, 256], P('prow'), may hold values from -1 to 2
- strip_inverse: bfloat16 [16, 256, 256], P('pcol'), may hold values from -1 to 2
- summit_inverse: bfloat16 [256, 256], replicated, may hold values from -1 to 2
- leaf_blocks: bfloat16 [16, 16, 28, 256, 256], P('prow', 'pcol'), may hold values from -0.09375 to 0.09375
- band_blocks: bfloat16 [16, 16, 8, 256, 256], P('prow', 'pcol'), may hold values from -0.0234375 to 0.0234375
- strip_blocks: bfloat16 [16, 16, 8, 256, 256], P('prow', 'pcol'), may hold values from -0.0234375 to 0.0234375
- summit_blocks: bfloat16 [16, 16, 8, 256, 256], P('prow', 'pcol'), may hold values from -0.015625 to 0.015625
- coupling: bfloat16 [16, 16, 256, 256], P('prow', 'pcol'), may hold values from -0.0625 to 0.0625
- summit_band: bfloat16 [16, 256, 256], P('prow', 'pcol'), may hold values from -0.046875 to 0.046875
- summit_strip: bfloat16 [16, 256, 256], P('pcol'), may hold values from -0.046875 to 0.046875
- parents: int32 [16, 16, 8], P('prow', 'pcol'), may hold values from 1 to 8, as said below
- widths: int32 [16, 16, 8], P('prow', 'pcol'), may hold values from 64 to 256
Outputs:
- leaf_answer: bfloat16 [16, 16, 8, 256, 128], P('prow', 'pcol')
- band_answer: bfloat16 [16, 256, 128], P('prow')
- strip_answer: bfloat16 [16, 256, 128], P('pcol')
- summit_answer: bfloat16 [256, 128], replicated
The draws below stay inside these ranges and needn't reach their ends.
Inputs may be any that keep to these rules, and one draw needn't show every extreme that they name: parents[r, c, a] is a later leaf of the same subtree, or 8 where leaf a links only to the separators.
All inputs are finite; a program needn't handle non-finite values.
Results may differ from the reference program's by a relative error of at most 0.015.
Values sent between devices are 32-bit elements; how exact they have to be, the bound alone decides.
A program may use at most 64 MiB of HBM per device.

```python
import math
import jax
import jax.numpy as jnp
from jax import lax

COLUMNS = 256
VECTORS = 128
LEAVES = 8
PASSES = 2
LEAF_PAIRS = 28
N_PROW = 16
N_PCOL = 16
DEVICES = 256


def inverse_stack(key, lead):
    shape = lead + (COLUMNS, COLUMNS)
    identity = jnp.eye(COLUMNS, dtype=jnp.float32)
    noise = jnp.clip(jax.random.normal(key, shape, jnp.float32), -4.0, 4.0) * (0.5 / math.sqrt(COLUMNS))
    return (identity + noise).astype(jnp.bfloat16)


def draw_leaf_inverse(key, part):
    return inverse_stack(key, (N_PROW, N_PCOL, LEAVES))


def draw_band_inverse(key, part):
    return inverse_stack(key, (N_PROW,))


def draw_strip_inverse(key, part):
    return inverse_stack(key, (N_PCOL,))


def draw_summit_inverse(key, part):
    return inverse_stack(key, ())


def draw_parents(key, part):
    positions = jnp.arange(LEAVES, dtype=jnp.int32)
    raw_bits = jax.random.randint(key, (N_PROW, N_PCOL, LEAVES), 0, 1 << 20, dtype=jnp.int32)
    return positions + 1 + raw_bits % (LEAVES - positions)


def set_ends(values, own_key, low, top_value):
    longest = values.shape.index(max(values.shape))
    spots = []
    for shift in (0, 1):
        where = [jax.random.randint(jax.random.fold_in(own_key, axis), (), 0, length) for axis, length in enumerate(values.shape)]
        where[longest] = (where[longest] + shift) % values.shape[longest]
        spots.append(tuple(where))
    return values.at[spots[0]].set(low).at[spots[1]].set(top_value)


def shard_levels(own_key, extent, shards, least, top_value):
    def one(dim, parts):
        steps = jax.random.uniform(jax.random.fold_in(jax.random.fold_in(own_key, 6), dim), (parts,), jnp.float32, least / len(shards), top_value / len(shards))
        return jnp.repeat(jnp.exp(steps), extent[dim] // parts).reshape((-1,) + (1,) * (len(extent) - dim - 1))

    level = one(*shards[0])
    for cut in shards[1:]:
        level = level * one(*cut)
    return level


def normal_values(own_key, dims, spread, most, split=(), held_as=jnp.bfloat16):
    drawn = spread * jax.random.normal(own_key, dims, jnp.float32)
    if split:
        drawn = drawn * shard_levels(own_key, dims, split, -0.22, 0.18)
    return jnp.clip(drawn, -most, most).astype(held_as)


def setup_inputs(seed: int = 0) -> dict:
    key_list = jax.random.split(jax.random.key(seed), 18)
    return {
        "leaf_source": normal_values(key_list[0], (N_PROW, N_PCOL, LEAVES, COLUMNS, VECTORS), 1.0, 6.0, ((0, 16), (1, 16))),
        "band_source": normal_values(key_list[1], (N_PROW, COLUMNS, VECTORS), 1.0, 6.0, ((0, 16),)),
        "strip_source": normal_values(key_list[2], (N_PCOL, COLUMNS, VECTORS), 1.0, 6.0, ((0, 16),)),
        "summit_source": normal_values(key_list[3], (COLUMNS, VECTORS), 1.0, 6.0),
        "leaf_inverse": draw_leaf_inverse(jax.random.fold_in(key_list[17], 71), 0),
        "band_inverse": draw_band_inverse(jax.random.fold_in(key_list[17], 71), 0),
        "strip_inverse": draw_strip_inverse(jax.random.fold_in(key_list[17], 71), 0),
        "summit_inverse": draw_summit_inverse(jax.random.fold_in(key_list[17], 71), 0),
        "leaf_blocks": normal_values(key_list[8], (N_PROW, N_PCOL, LEAF_PAIRS, COLUMNS, COLUMNS), (2 * COLUMNS * LEAVES) ** -0.5, 0.09375, ((0, 16), (1, 16))),
        "band_blocks": normal_values(key_list[9], (N_PROW, N_PCOL, LEAVES, COLUMNS, COLUMNS), (2 * COLUMNS * N_PCOL * LEAVES) ** -0.5, 0.0234375, ((0, 16), (1, 16))),
        "strip_blocks": normal_values(key_list[10], (N_PROW, N_PCOL, LEAVES, COLUMNS, COLUMNS), (2 * COLUMNS * N_PROW * LEAVES) ** -0.5, 0.0234375, ((0, 16), (1, 16))),
        "summit_blocks": normal_values(key_list[11], (N_PROW, N_PCOL, LEAVES, COLUMNS, COLUMNS), (COLUMNS * DEVICES * LEAVES // 4) ** -0.5, 0.015625, ((0, 16), (1, 16))),
        "coupling": normal_values(key_list[12], (N_PROW, N_PCOL, COLUMNS, COLUMNS), (2 * COLUMNS * N_PROW) ** -0.5, 0.0625, ((0, 16), (1, 16))),
        "summit_band": normal_values(key_list[13], (N_PROW, COLUMNS, COLUMNS), (2 * COLUMNS * (N_PROW + N_PCOL)) ** -0.5, 0.046875, ((0, 16), (1, 16))),
        "summit_strip": normal_values(key_list[14], (N_PCOL, COLUMNS, COLUMNS), (2 * COLUMNS * (N_PROW + N_PCOL)) ** -0.5, 0.046875, ((0, 16),)),
        "parents": draw_parents(jax.random.fold_in(key_list[17], 71), 0),
        "widths": set_ends(jax.random.randint(key_list[16], (N_PROW, N_PCOL, LEAVES), COLUMNS // 4, COLUMNS + 1), jax.random.fold_in(key_list[16], 1), COLUMNS // 4, COLUMNS).astype(jnp.int32),
    }


def ancestors(parent_list, leaf_count):
    node_ids = jnp.arange(leaf_count + 1, dtype=jnp.int32)
    current = parent_list.astype(jnp.int32)
    extended = jnp.concatenate([current, jnp.full((1,), leaf_count, jnp.int32)])
    reached = jnp.zeros((leaf_count + 1, leaf_count), jnp.float32)
    for repeat in range(leaf_count):
        matches = current[None, :] == node_ids[:, None]
        reached = jnp.maximum(reached, matches.astype(jnp.float32))
        current = jnp.sum(jnp.where(matches, extended[:, None], 0), axis=0).astype(jnp.int32)
    return reached[:leaf_count]


def product(left, right, form):
    return jnp.einsum(form, left.astype(jnp.float32), right.astype(jnp.float32), precision=lax.Precision.HIGHEST)


def forward_block(inverse, source, partial_value):
    residual = (source.astype(jnp.float32) - partial_value).astype(jnp.bfloat16)
    return product(inverse, residual, "ij,jr->ir").astype(jnp.bfloat16)


def backward_block(inverse, source, partial_value):
    residual = (source.astype(jnp.float32) - partial_value).astype(jnp.bfloat16)
    return product(inverse, residual, "ji,jr->ir").astype(jnp.bfloat16)


def leaf_forward(pair_blocks, inverses, sources, reached, row_mask):
    leaf_count = sources.shape[0]
    solved = []
    for position in range(leaf_count):
        residual = sources[position].astype(jnp.float32)
        if position > 0:
            first_pair = position * (position - 1) // 2
            weights = reached[position, :position]
            stacked = jnp.stack(solved).astype(jnp.float32) * weights[:, None, None]
            residual = residual - product(pair_blocks[first_pair:first_pair + position], stacked, "bij,bjr->ir")
        residual = (row_mask[position] * residual).astype(jnp.bfloat16)
        solved.append((row_mask[position] * product(inverses[position], residual, "ij,jr->ir")).astype(jnp.bfloat16))
    return jnp.stack(solved)


def leaf_backward(pair_blocks, inverses, solved, outer, reached, row_mask):
    leaf_count = solved.shape[0]
    pending = outer
    answers = [None] * leaf_count
    for position in reversed(range(leaf_count)):
        residual = (row_mask[position] * (solved[position].astype(jnp.float32) - pending[position])).astype(jnp.bfloat16)
        update = (row_mask[position] * product(inverses[position], residual, "ji,jr->ir")).astype(jnp.bfloat16)
        answers[position] = update
        if position > 0:
            first_pair = position * (position - 1) // 2
            pushed = product(pair_blocks[first_pair:first_pair + position], update, "bji,jr->bir")
            pending = pending.at[:position].add(reached[position, :position][:, None, None] * pushed)
    return jnp.stack(answers)


def reference(leaf_source, band_source, strip_source, summit_source, leaf_inverse, band_inverse, strip_inverse, summit_inverse, leaf_blocks, band_blocks, strip_blocks, summit_blocks, coupling, summit_band, summit_strip, parents, widths):
    grid_count = N_PROW * N_PCOL

    def flatten(array):
        return array.reshape((grid_count,) + array.shape[2:])

    column_ids = jnp.arange(COLUMNS, dtype=jnp.int32)

    def masks_of(width_list):
        return (column_ids[None, :] < width_list[:, None]).astype(jnp.float32)[:, :, None]

    leaf_inputs = tuple(flatten(array) for array in (leaf_inverse, leaf_blocks, band_blocks, strip_blocks, summit_blocks, parents, widths))
    current = (leaf_source, band_source, strip_source, summit_source)
    for iteration in range(PASSES):
        leaf_now, band_now, strip_now, summit_now = current

        def forward_one(items):
            inverse, pairs, to_band, to_strip, to_summit, parent_one, width_one, source = items
            reached = ancestors(parent_one, LEAVES)
            solved = leaf_forward(pairs, inverse, source, reached, masks_of(width_one))
            return (solved, product(to_band, solved, "aij,ajr->ir"), product(to_strip, solved, "aij,ajr->ir"), product(to_summit, solved, "aij,ajr->ir"))

        solved, band_terms, strip_terms, summit_terms = lax.map(forward_one, leaf_inputs + (flatten(leaf_now),))
        band_partial = band_terms.reshape(N_PROW, N_PCOL, COLUMNS, VECTORS).sum(axis=1)
        band_solved = jax.vmap(forward_block)(band_inverse, band_now, band_partial)
        strip_partial = strip_terms.reshape(N_PROW, N_PCOL, COLUMNS, VECTORS).sum(axis=0) + product(coupling, band_solved, "rcij,rjn->cin")
        strip_solved = jax.vmap(forward_block)(strip_inverse, strip_now, strip_partial)
        summit_partial = summit_terms.sum(axis=0) + product(summit_band, band_solved, "rki,rkn->in") + product(summit_strip, strip_solved, "cki,ckn->in")
        summit_solved = forward_block(summit_inverse, summit_now, summit_partial)
        summit_answer = backward_block(summit_inverse, summit_solved, jnp.zeros((COLUMNS, VECTORS), jnp.float32))
        strip_answer = jax.vmap(backward_block)(strip_inverse, strip_solved, product(summit_strip, summit_answer, "cki,in->ckn"))
        band_back = product(coupling, strip_answer, "rcji,cjn->rin") + product(summit_band, summit_answer, "rki,in->rkn")
        band_answer = jax.vmap(backward_block)(band_inverse, band_solved, band_back)
        band_each = jnp.broadcast_to(band_answer[:, None], (N_PROW, N_PCOL, COLUMNS, VECTORS)).reshape(grid_count, COLUMNS, VECTORS)
        strip_each = jnp.broadcast_to(strip_answer[None], (N_PROW, N_PCOL, COLUMNS, VECTORS)).reshape(grid_count, COLUMNS, VECTORS)

        def backward_one(items):
            inverse, pairs, to_band, to_strip, to_summit, parent_one, width_one, solved_one, band_one, strip_one = items
            reached = ancestors(parent_one, LEAVES)
            outer = product(to_band, band_one, "aij,ir->ajr") + product(to_strip, strip_one, "aij,ir->ajr") + product(to_summit, summit_answer, "aij,ir->ajr")
            return leaf_backward(pairs, inverse, solved_one, outer, reached, masks_of(width_one))

        leaf_answer = lax.map(backward_one, leaf_inputs + (solved, band_each, strip_each)).reshape(leaf_source.shape)
        current = (leaf_answer, band_answer, strip_answer, summit_answer)
    return current[0], current[1], current[2], current[3]
```

```python
import functools

import jax
import jax.numpy as jnp
from jax import lax
from jax.experimental import pallas as pl
from jax.experimental.pallas import tpu as pltpu
from jax.sharding import PartitionSpec as P

PASSES = 2
MESH = pl.DeviceIdType.MESH
F32 = jnp.float32
BF16 = jnp.bfloat16


def nn(left, right):
    return jnp.dot(left, right, preferred_element_type=F32)


def nt(left, right):
    return lax.dot_general(left, right, (((1,), (1,)), ((), ())), preferred_element_type=F32)


def pair(a, b):
    return a * (a - 1) // 2 + b


def kernel(
    rows,
    cols,
    parents,
    widths,
    leaf_source,
    band_source,
    strip_source,
    summit_source,
    leaf_inverse,
    band_inverse,
    strip_inverse,
    summit_inverse,
    leaf_blocks,
    band_blocks,
    strip_blocks,
    summit_blocks,
    coupling,
    summit_band,
    summit_strip,
    leaf_out,
    band_out,
    strip_out,
    summit_out,
    source_in,
    border_in,
    linv,
    lblk,
    bblk,
    sblk,
    mblk,
    link,
    binv,
    sinv,
    uinv,
    lift_in,
    lift,
    slift,
    now,
    solved,
    pend,
    band_src,
    strip_src,
    summit_src,
    send1,
    send3,
    send6,
    land1,
    land2,
    land3,
    land4,
    land5,
    land6,
    land7,
    band_hold,
    load_sem,
    send_sem,
    recv_sem,
):
    leaves, size, count = leaf_source.shape
    r = lax.axis_index("prow")
    c = lax.axis_index("pcol")
    band_rhs = count // cols
    strip_rhs = count // rows

    loads = [
        (leaf_source, source_in),
        (leaf_inverse, linv),
        (leaf_blocks, lblk),
        (band_blocks, bblk),
        (strip_blocks, sblk),
        (summit_blocks, mblk),
        (band_source, border_in.at[0]),
        (strip_source, border_in.at[1]),
        (summit_source, border_in.at[2]),
        (coupling, link),
        (band_inverse, binv),
        (strip_inverse, sinv),
        (summit_inverse, uinv),
        (summit_band, lift_in),
        (summit_strip, slift),
    ]
    copies = [
        pltpu.make_async_copy(src, dst, load_sem.at[place])
        for place, (src, dst) in enumerate(loads)
    ]
    for copy in copies:
        copy.start()

    barrier = pltpu.get_barrier_semaphore()

    def greet_col(k, carry):
        pl.semaphore_signal(
            barrier, inc=1, device_id=(r, lax.rem(c + k, cols)), device_id_type=MESH
        )
        return carry

    def greet_row(k, carry):
        pl.semaphore_signal(
            barrier, inc=1, device_id=(lax.rem(r + k, rows), c), device_id_type=MESH
        )
        return carry

    lax.fori_loop(1, cols, greet_col, 0)
    lax.fori_loop(1, rows, greet_row, 0)

    def reach_of():
        parent = [parents[b] for b in range(leaves)]
        reach = {}
        for a in range(leaves):
            for b in reversed(range(a)):
                met = (parent[b] == a).astype(jnp.int32)
                for k in range(b + 1, a):
                    met = met + (parent[b] == k).astype(jnp.int32) * reach[a, k]
                reach[a, b] = met
        return reach

    reach = reach_of()

    copies[0].wait()
    for a in range(leaves):
        now[a] = source_in[a].astype(F32).T.astype(BF16)
    copies[1].wait()
    down = lax.broadcasted_iota(jnp.int32, (size, size), 0)
    across = lax.broadcasted_iota(jnp.int32, (size, size), 1)
    furthest = jnp.maximum(down, across)
    for a in range(leaves):
        linv[a] = jnp.where(furthest < widths[a], linv[a].astype(F32), 0.0).astype(BF16)
    copies[2].wait()
    for a in range(leaves):
        for b in range(a):
            weight = reach[a, b].astype(F32)
            lblk[pair(a, b)] = (lblk[pair(a, b)].astype(F32) * weight).astype(BF16)
    for copy in copies[3:]:
        copy.wait()
    send1[...] = border_in[0].astype(F32).T.reshape(send1.shape)
    band_src[...] = send1[c]
    send3[:, 0] = border_in[1].astype(F32).T.reshape(rows, strip_rhs, size)
    send3[:, 1] = border_in[2].astype(F32).T.reshape(rows, strip_rhs, size)
    strip_src[...] = send3[r, 0]
    summit_src[...] = send3[r, 1]
    lift[...] = jnp.zeros_like(lift)
    slab = lift_in.shape[0]
    lift[pl.ds(pl.multiple_of(c * slab, slab), slab), :] = lift_in[...]

    def col_copy(p, phase, src, dst, other):
        return pltpu.make_async_remote_copy(
            src_ref=src,
            dst_ref=dst,
            send_sem=send_sem.at[p, phase],
            recv_sem=recv_sem.at[p, phase],
            device_id=(r, other),
            device_id_type=MESH,
        )

    def row_copy(p, phase, src, dst, other):
        return pltpu.make_async_remote_copy(
            src_ref=src,
            dst_ref=dst,
            send_sem=send_sem.at[p, phase],
            recv_sem=recv_sem.at[p, phase],
            device_id=(other, c),
            device_id_type=MESH,
        )

    def scatter(make, p, phase, me, n, source, land):
        def step(k, carry):
            other = lax.rem(me + k, n)
            make(p, phase, source.at[other], land.at[p, me], other).start()
            return carry

        lax.fori_loop(1, n, step, 0)
        land[p, me] = source[me]

    def spread(make, p, phase, me, n, land):
        def step(k, carry):
            other = lax.rem(me + k, n)
            make(p, phase, land.at[p, me], land.at[p, me], other).start()
            return carry

        lax.fori_loop(1, n, step, 0)

    def finish(make, p, phase, n, land):
        part = land.at[p, pl.ds(0, n - 1)]
        copy = make(p, phase, part, part, 0)
        copy.wait_recv()
        copy.wait_send()

    def total(values):
        values = [values[k] for k in range(values.shape[0])]
        while len(values) > 1:
            values = [
                values[k] + values[k + 1] if k + 1 < len(values) else values[k]
                for k in range(0, len(values), 2)
            ]
        return values[0]

    def full(value):
        return value.reshape(count, size).astype(BF16)

    def one_pass(p, carry):
        for a in range(leaves):
            pend[a] = now[a].astype(F32)
        for b in range(leaves):
            answer = nt(pend[b].astype(BF16), linv[b]).astype(BF16)
            solved[b] = answer
            for a in range(b + 1, leaves):
                pend[a] -= nt(answer, lblk[pair(a, b)])

        def term(blocks):
            result = nt(solved[0], blocks[0])
            for a in range(1, leaves):
                result = result + nt(solved[a], blocks[a])
            return result

        send1[...] = term(bblk).reshape(send1.shape)

        @pl.when(p == 0)
        def _():
            pl.semaphore_wait(barrier, rows + cols - 2)

        scatter(col_copy, p, 0, c, cols, send1, land1)
        strip_term = term(sblk)
        finish(col_copy, p, 0, cols, land1)
        rest = (band_src[...] - total(land1[p])).astype(BF16)
        band_slab = nt(rest, binv[...]).astype(BF16).astype(F32)
        band_hold[...] = band_slab
        land2[p, c] = band_slab
        spread(col_copy, p, 1, c, cols, land2)
        summit_term = term(mblk)
        finish(col_copy, p, 1, cols, land2)
        band_solved = full(land2[p])
        send3[:, 0] = (strip_term + nt(band_solved, link[...])).reshape(rows, strip_rhs, size)
        send3[:, 1] = (summit_term + nn(band_solved, lift[...])).reshape(rows, strip_rhs, size)
        scatter(row_copy, p, 2, r, rows, send3, land3)
        finish(row_copy, p, 2, rows, land3)
        sums = total(land3[p])
        strip_slab = nt((strip_src[...] - sums[0]).astype(BF16), sinv[...]).astype(BF16)
        land4[p, c] = sums[1] + nn(strip_slab, slift[...])
        spread(col_copy, p, 3, c, cols, land4)
        finish(col_copy, p, 3, cols, land4)
        top = nt((summit_src[...] - total(land4[p])).astype(BF16), uinv[...]).astype(BF16)
        top_answer = nn(top, uinv[...]).astype(BF16)
        rest = (strip_slab.astype(F32) - nt(top_answer, slift[...])).astype(BF16)
        strip_answer = nn(rest, sinv[...]).astype(BF16).astype(F32)
        top_answer = top_answer.astype(F32)
        strip_src[...] = strip_answer
        summit_src[...] = top_answer
        land5[p, r, 0] = strip_answer
        land5[p, r, 1] = top_answer
        spread(row_copy, p, 4, r, rows, land5)
        finish(row_copy, p, 4, rows, land5)
        strip_all = full(land5[p, :, 0])
        top_all = full(land5[p, :, 1])
        send6[...] = (nn(strip_all, link[...]) + nt(top_all, lift[...])).reshape(send6.shape)
        scatter(col_copy, p, 5, c, cols, send6, land6)
        for a in range(leaves):
            pend[a] = solved[a].astype(F32) - (nn(strip_all, sblk[a]) + nn(top_all, mblk[a]))
        finish(col_copy, p, 5, cols, land6)
        rest = (band_hold[...] - total(land6[p])).astype(BF16)
        band_answer = nn(rest, binv[...]).astype(BF16).astype(F32)
        band_src[...] = band_answer
        land7[p, c] = band_answer
        spread(col_copy, p, 6, c, cols, land7)
        finish(col_copy, p, 6, cols, land7)
        band_all = full(land7[p])
        for a in reversed(range(leaves)):
            pend[a] -= nn(band_all, bblk[a])
        for a in reversed(range(leaves)):
            answer = nn(pend[a].astype(BF16), linv[a]).astype(BF16)
            now[a] = answer
            for b in reversed(range(a)):
                pend[b] -= nn(answer, lblk[pair(a, b)])
        return carry

    lax.fori_loop(0, PASSES, one_pass, 0)
    last = PASSES - 1
    for a in range(leaves):
        leaf_out[a] = now[a].astype(F32).T.astype(BF16)
    band_out[...] = land7[last].reshape(count, size).T.astype(BF16)
    strip_out[...] = land5[last, :, 0].reshape(count, size).T.astype(BF16)
    summit_out[...] = land5[last, :, 1].reshape(count, size).T.astype(BF16)


def per_device(
    rows,
    cols,
    leaf_source,
    band_source,
    strip_source,
    summit_source,
    leaf_inverse,
    band_inverse,
    strip_inverse,
    summit_inverse,
    leaf_blocks,
    band_blocks,
    strip_blocks,
    summit_blocks,
    coupling,
    summit_band,
    summit_strip,
    parents,
    widths,
):
    leaves, size, count = leaf_source.shape[2:]
    pairs = leaf_blocks.shape[2]
    slab = summit_band.shape[1]
    band_rhs = count // cols
    strip_rhs = count // rows
    square = (size, size)
    anywhere = pl.BlockSpec(memory_space=pl.ANY)
    scalars = pl.BlockSpec(memory_space=pltpu.SMEM)
    vmem = pl.BlockSpec(memory_space=pltpu.VMEM)
    results = pl.pallas_call(
        functools.partial(kernel, rows, cols),
        out_shape=(
            jax.ShapeDtypeStruct((leaves, size, count), BF16),
            jax.ShapeDtypeStruct((size, count), BF16),
            jax.ShapeDtypeStruct((size, count), BF16),
            jax.ShapeDtypeStruct((size, count), BF16),
        ),
        in_specs=[scalars] * 2 + [anywhere] * 15,
        out_specs=(vmem,) * 4,
        scratch_shapes=[
            pltpu.VMEM((leaves, size, count), BF16),
            pltpu.VMEM((3, size, count), BF16),
            pltpu.VMEM((leaves,) + square, BF16),
            pltpu.VMEM((pairs,) + square, BF16),
            pltpu.VMEM((leaves,) + square, BF16),
            pltpu.VMEM((leaves,) + square, BF16),
            pltpu.VMEM((leaves,) + square, BF16),
            pltpu.VMEM(square, BF16),
            pltpu.VMEM(square, BF16),
            pltpu.VMEM(square, BF16),
            pltpu.VMEM(square, BF16),
            pltpu.VMEM((slab, size), BF16),
            pltpu.VMEM(square, BF16),
            pltpu.VMEM(square, BF16),
            pltpu.VMEM((leaves, count, size), BF16),
            pltpu.VMEM((leaves, count, size), BF16),
            pltpu.VMEM((leaves, count, size), F32),
            pltpu.VMEM((band_rhs, size), F32),
            pltpu.VMEM((strip_rhs, size), F32),
            pltpu.VMEM((strip_rhs, size), F32),
            pltpu.VMEM((cols, band_rhs, size), F32),
            pltpu.VMEM((rows, 2, strip_rhs, size), F32),
            pltpu.VMEM((cols, band_rhs, size), F32),
            pltpu.VMEM((PASSES, cols, band_rhs, size), F32),
            pltpu.VMEM((PASSES, cols, band_rhs, size), F32),
            pltpu.VMEM((PASSES, rows, 2, strip_rhs, size), F32),
            pltpu.VMEM((PASSES, cols, strip_rhs, size), F32),
            pltpu.VMEM((PASSES, rows, 2, strip_rhs, size), F32),
            pltpu.VMEM((PASSES, cols, band_rhs, size), F32),
            pltpu.VMEM((PASSES, cols, band_rhs, size), F32),
            pltpu.VMEM((band_rhs, size), F32),
            pltpu.SemaphoreType.DMA((15,)),
            pltpu.SemaphoreType.DMA((PASSES, 7)),
            pltpu.SemaphoreType.DMA((PASSES, 7)),
        ],
        compiler_params=pltpu.CompilerParams(
            collective_id=0, has_side_effects=True, vmem_limit_bytes=56 * 1024 * 1024
        ),
        cost_estimate=pl.CostEstimate(
            flops=4_400_000_000, bytes_accessed=10_000_000, transcendentals=0
        ),
    )(
        parents[0, 0],
        widths[0, 0],
        leaf_source[0, 0],
        band_source[0],
        strip_source[0],
        summit_source,
        leaf_inverse[0, 0],
        band_inverse[0],
        strip_inverse[0],
        summit_inverse,
        leaf_blocks[0, 0],
        band_blocks[0, 0],
        strip_blocks[0, 0],
        summit_blocks[0, 0],
        coupling[0, 0],
        summit_band[0],
        summit_strip[0],
    )
    return results[0][None, None], results[1][None], results[2][None], results[3]


def solution(mesh):
    placed = (
        P("prow", "pcol", None, None, None),
        P("prow", None, None),
        P("pcol", None, None),
        P(),
        P("prow", "pcol", None, None, None),
        P("prow", None, None),
        P("pcol", None, None),
        P(),
        P("prow", "pcol", None, None, None),
        P("prow", "pcol", None, None, None),
        P("prow", "pcol", None, None, None),
        P("prow", "pcol", None, None, None),
        P("prow", "pcol", None, None),
        P("prow", "pcol", None),
        P("pcol", None, None),
        P("prow", "pcol", None),
        P("prow", "pcol", None),
    )
    return jax.shard_map(
        functools.partial(per_device, mesh.shape["prow"], mesh.shape["pcol"]),
        mesh=mesh,
        in_specs=placed,
        out_specs=(
            P("prow", "pcol", None, None, None),
            P("prow", None, None),
            P("pcol", None, None),
            P(),
        ),
        check_vma=False,
    )
```

```python
import functools

import jax
import jax.numpy as jnp
from jax import lax
from jax.experimental import pallas as pl
from jax.experimental.pallas import tpu as pltpu
from jax.sharding import PartitionSpec as P

PASSES = 2
MESH = pl.DeviceIdType.MESH
F32 = jnp.float32
BF16 = jnp.bfloat16


def nn(left, right):
    return jnp.dot(left, right, preferred_element_type=F32)


def nt(left, right):
    return lax.dot_general(left, right, (((1,), (1,)), ((), ())), preferred_element_type=F32)


def pair(a, b):
    return a * (a - 1) // 2 + b


def kernel(
    rows,
    cols,
    parents,
    widths,
    leaf_source,
    band_source,
    strip_source,
    summit_source,
    leaf_inverse,
    band_inverse,
    strip_inverse,
    summit_inverse,
    leaf_blocks,
    band_blocks,
    strip_blocks,
    summit_blocks,
    coupling,
    summit_band,
    summit_strip,
    leaf_out,
    border_out,
    source_in,
    border_in,
    linv,
    lblk,
    stack,
    keys,
    link,
    binv,
    sinv,
    uinv,
    lift_in,
    lift,
    slift,
    lowered,
    joined,
    now,
    solved,
    pend,
    slabs,
    sends,
    send_mats,
    send_pair,
    lands,
    land_mats,
    land_pair,
    load_sem,
    send_sem,
    recv_sem,
):
    leaves, size, count = leaf_source.shape
    r = lax.axis_index("prow")
    c = lax.axis_index("pcol")

    side = int(round(cols**0.5))
    chips = rows // 2

    def away(step, n):
        return min(step, n - step)

    col_steps = sorted(
        range(1, cols), key=lambda k: -away(k // side, side) - away(k % side, side)
    )
    row_steps = sorted(range(1, rows), key=lambda k: -away(k // 2, chips))
    col_peers = [
        (r, lax.rem(c // side + k // side, side) * side + lax.rem(c % side + k % side, side))
        for k in col_steps
    ]
    row_peers = [
        (lax.rem(r // 2 + k // 2, chips) * 2 + lax.rem(r % 2 + k % 2, 2), c) for k in row_steps
    ]
    along_cols = (1, c, col_peers)
    along_rows = (0, r, row_peers)

    def whole(place):
        return stack.at[:, pl.ds(place * size, size), :]

    loads = [(leaf_source, source_in), (leaf_inverse, linv)]
    for a in range(1, leaves):
        part = pl.ds(pair(a, 0), a)
        loads.append((leaf_blocks.at[part], lblk.at[part]))
    loads += [
        (band_blocks, whole(0)),
        (strip_blocks, whole(1)),
        (summit_blocks, whole(2)),
        (band_source, border_in.at[0]),
        (strip_source, border_in.at[1]),
        (summit_source, border_in.at[2]),
        (coupling, link),
        (band_inverse, binv),
        (strip_inverse, sinv),
        (summit_inverse, uinv),
        (summit_band, lift_in),
        (summit_strip, slift),
    ]
    copies = [
        pltpu.make_async_copy(src, dst, load_sem.at[place])
        for place, (src, dst) in enumerate(loads)
    ]
    for copy in copies:
        copy.start()

    barrier = pltpu.get_barrier_semaphore()
    for peer in col_peers + row_peers:
        pl.semaphore_signal(barrier, inc=1, device_id=peer, device_id_type=MESH)

    parent = [parents[b] for b in range(leaves)]
    reach = {}
    for a in range(leaves):
        for b in reversed(range(a)):
            met = (parent[b] == a).astype(jnp.int32)
            for k in range(b + 1, a):
                met = met + (parent[b] == k).astype(jnp.int32) * reach[a, k]
            reach[a, b] = met
    down = lax.broadcasted_iota(jnp.int32, (size, size), 0)
    across = lax.broadcasted_iota(jnp.int32, (size, size), 1)
    furthest = jnp.maximum(down, across)

    def prepare(a):
        linv[a] = jnp.where(furthest < widths[a], linv[a].astype(F32), 0.0).astype(BF16)
        now[a] = source_in[a].astype(F32).T.astype(BF16)
        for b in range(a):
            weight = reach[a, b].astype(F32)
            lblk[pair(a, b)] = (lblk[pair(a, b)].astype(F32) * weight).astype(BF16)

    used = []

    def ship(make_src, make_dst, peers, phase):
        for peer in peers:
            pltpu.make_async_remote_copy(
                src_ref=make_src(peer),
                dst_ref=make_dst(peer),
                send_sem=send_sem.at[phase],
                recv_sem=recv_sem.at[phase],
                device_id=peer,
                device_id_type=MESH,
            ).start()

    def scatter(axis, phase, source, land):
        dim, me, peers = axis
        ship(lambda peer: source.at[peer[dim]], lambda peer: land.at[me], peers, phase)
        land[me] = source[me]
        used.append((peers, land, phase))

    def spread(axis, phase, value, land):
        dim, me, peers = axis
        land[me] = value
        ship(lambda peer: land.at[me], lambda peer: land.at[me], peers, phase)
        used.append((peers, land, phase))

    def bytes_of(peers, land, phase):
        part = land.at[pl.ds(0, len(peers))]
        return pltpu.make_async_remote_copy(
            src_ref=part,
            dst_ref=part,
            send_sem=send_sem.at[phase],
            recv_sem=recv_sem.at[phase],
            device_id=peers[0],
            device_id_type=MESH,
        )

    def finish(axis, phase, land):
        bytes_of(axis[2], land, phase).wait_recv()

    def total(values):
        values = [values[k] for k in range(values.shape[0])]
        while len(values) > 1:
            values = [
                values[k] + values[k + 1] if k + 1 < len(values) else values[k]
                for k in range(0, len(values), 2)
            ]
        return values[0]

    def full(value):
        return value.reshape(count, size).astype(BF16)

    def parts(value, n):
        return value.reshape(n, count // n, size)

    def rounded(value):
        return value.astype(BF16).astype(F32)

    def forward_step(a):
        rest = now[a].astype(F32)
        for b in range(a):
            rest = rest - nt(solved[b], lblk[pair(a, b)])
        solved[a] = nt(rest.astype(BF16), linv[a]).astype(BF16)

    def backward_chain():
        for a in reversed(range(leaves)):
            rest = solved[a].astype(F32)
            for b in range(a + 1, leaves):
                rest = rest - nn(solved[b], lblk[pair(b, a)])
            answer = nn(rest.astype(BF16), linv[a])
            pend[a] = answer
            solved[a] = answer.astype(BF16)

    def term(values, blocks, place):
        part = pl.ds(place * size, size)
        result = nt(values[0], blocks[0, part, :])
        for a in range(1, leaves):
            result = result + nt(values[a], blocks[a, part, :])
        return result

    copies[0].wait()
    copies[1].wait()
    prepare(0)
    for a in range(leaves):
        if a + 1 < leaves:
            copies[2 + a].wait()
            prepare(a + 1)
        forward_step(a)
    for copy in copies[leaves + 1 :]:
        copy.wait()
    sends[0] = parts(term(solved, stack, 0), cols)
    pl.semaphore_wait(barrier, rows + cols - 2)
    scatter(along_cols, 0, sends.at[0], lands.at[0])

    strip_term = term(solved, stack, 1)
    summit_term = term(solved, stack, 2)
    slabs[0] = parts(border_in[0].astype(F32).T, cols)
    slabs[1] = parts(border_in[1].astype(F32).T, rows)
    slabs[2] = parts(border_in[2].astype(F32).T, cols)
    band_src = slabs[0, c]
    strip_src = slabs[1, r]
    summit_src = slabs[2, c]
    strip_now = slabs[1].reshape(count, size)
    lift[...] = jnp.zeros_like(lift)
    slab = lift_in.shape[0]
    lift[pl.ds(pl.multiple_of(c * slab, slab), slab), :] = lift_in[...]
    turned = sinv[...].astype(F32).T.astype(BF16)
    lowered[...] = nn(turned, slift[...]).astype(BF16)
    joined[...] = nn(sinv[...], link[...]).astype(BF16)
    turned = link[...].astype(F32).T.astype(BF16)
    send_mats[:, 0] = (nn(turned, lowered[...]) - lift[...].astype(F32)).reshape(cols, slab, size)

    def key_step(a):
        rest = stack[a].astype(F32)
        for b in range(a + 1, leaves):
            rest = rest - nn(keys[b], lblk[pair(b, a)])
        keys[a] = nn(rest.astype(BF16), linv[a]).astype(BF16)

    half = leaves // 2
    for a in reversed(range(half, leaves)):
        key_step(a)
    finish(along_cols, 0, lands.at[0])
    rest = band_src - total(lands[0])
    band_slab = rounded(nt(rest.astype(BF16), binv[...]))
    spread(along_cols, 1, band_slab, lands.at[1])
    for a in reversed(range(half)):
        key_step(a)
    cross = nt(keys[0, pl.ds(0, size), :], keys[0])
    for a in range(1, leaves):
        cross = cross + nt(keys[a, pl.ds(0, size), :], keys[a])
    band_strip = cross[:, size : 2 * size].astype(BF16)
    send_mats[:, 1] = cross[:, :size].reshape(cols, slab, size)
    send_mats[:, 2] = (nn(band_strip, lowered[...]) - cross[:, 2 * size :]).reshape(
        cols, slab, size
    )
    finish(along_cols, 1, lands.at[1])
    band_all = full(lands[1])

    mats = None
    for p in range(PASSES):
        first = p == 0
        base = 2 + 7 * p
        pushed = strip_term + nt(band_all, link[...])
        sends[base] = parts(pushed, rows)
        scatter(along_rows, base, sends.at[base], lands.at[base])
        spare = (strip_now * (1.0 / rows) - pushed).astype(BF16)
        if not first:
            summit_term = term(now, keys, 2)
        raised = summit_term + nn(band_all, lift[...]) + nn(spare, lowered[...])
        sends[base + 1] = parts(raised, cols)
        scatter(along_cols, base + 1, sends.at[base + 1], lands.at[base + 1])
        if first:
            mat_phase = 2 + 7 * PASSES
            scatter(along_cols, mat_phase, send_mats, land_mats.at[0])
        else:
            for a in range(leaves):
                forward_step(a)
        backward_chain()
        finish(along_rows, base, lands.at[base])
        rest = strip_src - total(lands[base])
        strip_slab = rounded(nt(rest.astype(BF16), sinv[...]))
        spread(along_rows, base + 2, strip_slab, lands.at[base + 2])
        finish(along_cols, base + 1, lands.at[base + 1])
        spread(along_rows, base + 3, total(lands[base + 1]), lands.at[base + 3])
        if first:
            finish(along_cols, mat_phase, land_mats.at[0])
            spread(along_cols, mat_phase + 1, total(land_mats[0]), land_mats.at[1])
            next_term = term(solved, keys, 0)
        finish(along_rows, base + 2, lands.at[base + 2])
        strip_all = full(lands[base + 2])
        dropped = nn(strip_all, joined[...])
        strip_own = nn(strip_all, sinv[...])
        if first:
            send_pair[:, 0] = parts(dropped, cols)
            send_pair[:, 1] = parts(next_term - nt(strip_own.astype(BF16), band_strip), cols)
            scatter(along_cols, base + 4, send_pair, land_pair.at[0])
        else:
            sends[base + 4] = parts(dropped, cols)
            scatter(along_cols, base + 4, sends.at[base + 4], lands.at[base + 4])
        finish(along_rows, base + 3, lands.at[base + 3])
        rest = summit_src - total(lands[base + 3])
        top = nt(rest.astype(BF16), uinv[...]).astype(BF16)
        top = nn(top, uinv[...]).astype(BF16)
        summit_src = top.astype(F32)
        spread(along_cols, base + 5, summit_src, lands.at[base + 5])
        if first:
            finish(along_cols, mat_phase + 1, land_mats.at[1])
            mats = [land_mats[1, :, k].reshape(size, size).astype(BF16) for k in range(3)]
            lblk_back = nt(top, mats[2])
        back = nt(top, mats[0])
        if first:
            finish(along_cols, base + 4, land_pair.at[0])
            sums = total(land_pair[0])
            rest = band_slab - sums[0] + back
            band_answer = nn(rest.astype(BF16), binv[...]).astype(BF16)
            rest = band_answer.astype(F32) - sums[1] + nt(band_answer, mats[1]) - lblk_back
            band_slab = rounded(nt(rest.astype(BF16), binv[...]))
            both = jnp.stack([band_answer.astype(F32), band_slab])
            spread(along_cols, base + 6, both, land_pair.at[1])
        else:
            finish(along_cols, base + 4, lands.at[base + 4])
            rest = band_slab - total(lands[base + 4]) + back
            band_answer = rounded(nn(rest.astype(BF16), binv[...]))
            spread(along_cols, base + 6, band_answer, lands.at[base + 6])
        finish(along_cols, base + 5, lands.at[base + 5])
        top_all = full(lands[base + 5])
        strip_answer = (strip_own - nt(top_all, lowered[...])).astype(BF16)
        strip_now = strip_answer.astype(F32)
        if first:
            slabs[1] = parts(strip_now, rows)
            strip_src = slabs[1, r]
        upper = jnp.concatenate([strip_answer, top_all], axis=1)
        lower_rows = pl.ds(size, 2 * size)
        for a in range(leaves):
            pend[a] -= nn(upper, keys[a, lower_rows, :])
        if first:
            finish(along_cols, base + 6, land_pair.at[1])
            band_full = full(land_pair[1, :, 0])
            band_all = full(land_pair[1, :, 1])
        else:
            finish(along_cols, base + 6, lands.at[base + 6])
            band_full = full(lands[base + 6])
        place = pl.ds(0, size)
        for a in range(leaves):
            value = (pend[a] - nn(band_full, keys[a, place, :])).astype(BF16)
            if first:
                now[a] = value
            else:
                leaf_out[a] = value
        if first:
            strip_term = term(now, keys, 1)
    border_out[0] = band_full
    border_out[1] = strip_answer
    border_out[2] = top_all
    for peers, land, phase in used:
        bytes_of(peers, land, phase).wait_send()


def turn(leaf_in, border_in, leaf_out, band_out, strip_out, summit_out):
    for a in range(leaf_in.shape[0]):
        leaf_out[a] = leaf_in[a].astype(F32).T.astype(BF16)
    for place, out in enumerate((band_out, strip_out, summit_out)):
        out[...] = border_in[place].astype(F32).T.astype(BF16)


def per_device(
    rows,
    cols,
    leaf_source,
    band_source,
    strip_source,
    summit_source,
    leaf_inverse,
    band_inverse,
    strip_inverse,
    summit_inverse,
    leaf_blocks,
    band_blocks,
    strip_blocks,
    summit_blocks,
    coupling,
    summit_band,
    summit_strip,
    parents,
    widths,
):
    leaves, size, count = leaf_source.shape[2:]
    pairs = leaf_blocks.shape[2]
    slab = summit_band.shape[1]
    band_rhs = count // cols
    square = (size, size)
    anywhere = pl.BlockSpec(memory_space=pl.ANY)
    scalars = pl.BlockSpec(memory_space=pltpu.SMEM)
    vmem = pl.BlockSpec(memory_space=pltpu.VMEM)
    plain = pltpu.VMEM(square, BF16)
    phases = 4 + 7 * PASSES
    solved = pl.pallas_call(
        functools.partial(kernel, rows, cols),
        out_shape=(
            jax.ShapeDtypeStruct((leaves, count, size), BF16),
            jax.ShapeDtypeStruct((3, count, size), BF16),
        ),
        in_specs=[scalars] * 2 + [anywhere] * 15,
        out_specs=(vmem,) * 2,
        scratch_shapes=[
            pltpu.VMEM((leaves, size, count), BF16),
            pltpu.VMEM((3, size, count), BF16),
            pltpu.VMEM((leaves,) + square, BF16),
            pltpu.VMEM((pairs,) + square, BF16),
            pltpu.VMEM((leaves, 3 * size, size), BF16),
            pltpu.VMEM((leaves, 3 * size, size), BF16),
            plain,
            plain,
            plain,
            plain,
            pltpu.VMEM((slab, size), BF16),
            plain,
            plain,
            plain,
            plain,
            pltpu.VMEM((leaves, count, size), BF16),
            pltpu.VMEM((leaves, count, size), BF16),
            pltpu.VMEM((leaves, count, size), F32),
            pltpu.VMEM((3, cols, band_rhs, size), F32),
            pltpu.VMEM((phases, cols, band_rhs, size), F32),
            pltpu.VMEM((cols, 3, slab, size), F32),
            pltpu.VMEM((cols, 2, band_rhs, size), F32),
            pltpu.VMEM((phases, cols, band_rhs, size), F32),
            pltpu.VMEM((2, cols, 3, slab, size), F32),
            pltpu.VMEM((2, cols, 2, band_rhs, size), F32),
            pltpu.SemaphoreType.DMA((32,)),
            pltpu.SemaphoreType.DMA((phases,)),
            pltpu.SemaphoreType.DMA((phases,)),
        ],
        compiler_params=pltpu.CompilerParams(
            collective_id=0, has_side_effects=True, vmem_limit_bytes=56 * 1024 * 1024
        ),
        cost_estimate=pl.CostEstimate(
            flops=4_400_000_000, bytes_accessed=10_000_000, transcendentals=0
        ),
    )(
        parents[0, 0],
        widths[0, 0],
        leaf_source[0, 0],
        band_source[0],
        strip_source[0],
        summit_source,
        leaf_inverse[0, 0],
        band_inverse[0],
        strip_inverse[0],
        summit_inverse,
        leaf_blocks[0, 0],
        band_blocks[0, 0],
        strip_blocks[0, 0],
        summit_blocks[0, 0],
        coupling[0, 0],
        summit_band[0],
        summit_strip[0],
    )
    results = pl.pallas_call(
        turn,
        out_shape=(
            jax.ShapeDtypeStruct((leaves, size, count), BF16),
            jax.ShapeDtypeStruct((size, count), BF16),
            jax.ShapeDtypeStruct((size, count), BF16),
            jax.ShapeDtypeStruct((size, count), BF16),
        ),
        in_specs=[vmem] * 2,
        out_specs=(vmem,) * 4,
    )(*solved)
    return results[0][None, None], results[1][None], results[2][None], results[3]


def solution(mesh):
    placed = (
        P("prow", "pcol", None, None, None),
        P("prow", None, None),
        P("pcol", None, None),
        P(),
        P("prow", "pcol", None, None, None),
        P("prow", None, None),
        P("pcol", None, None),
        P(),
        P("prow", "pcol", None, None, None),
        P("prow", "pcol", None, None, None),
        P("prow", "pcol", None, None, None),
        P("prow", "pcol", None, None, None),
        P("prow", "pcol", None, None),
        P("prow", "pcol", None),
        P("pcol", None, None),
        P("prow", "pcol", None),
        P("prow", "pcol", None),
    )
    return jax.shard_map(
        functools.partial(per_device, mesh.shape["prow"], mesh.shape["pcol"]),
        mesh=mesh,
        in_specs=placed,
        out_specs=(
            P("prow", "pcol", None, None, None),
            P("prow", None, None),
            P("pcol", None, None),
            P(),
        ),
        check_vma=False,
    )
```

```python
import functools

import jax
import jax.numpy as jnp
from jax import lax
from jax.experimental import pallas as pl
from jax.experimental.pallas import tpu as pltpu
from jax.sharding import PartitionSpec as P

PASSES = 2
MESH = pl.DeviceIdType.MESH
F32 = jnp.float32
BF16 = jnp.bfloat16


def nn(left, right):
    return jnp.dot(left, right, preferred_element_type=F32)


def nt(left, right):
    return lax.dot_general(left, right, (((1,), (1,)), ((), ())), preferred_element_type=F32)


def pair(a, b):
    return a * (a - 1) // 2 + b


def kernel(
    rows,
    cols,
    parents,
    widths,
    leaf_source,
    band_source,
    strip_source,
    summit_source,
    leaf_inverse,
    band_inverse,
    strip_inverse,
    summit_inverse,
    leaf_blocks,
    band_blocks,
    strip_blocks,
    summit_blocks,
    coupling,
    summit_band,
    summit_strip,
    leaf_out,
    border_out,
    source_in,
    border_in,
    linv,
    lblk,
    bridge,
    stack,
    keys,
    link,
    binv,
    sinv,
    uinv,
    lift_in,
    lift,
    slift,
    lowered,
    joined,
    now,
    solved,
    pend,
    slabs,
    sends,
    send_mat,
    send_mats,
    send_pair,
    lands,
    land_mat,
    land_mats,
    land_pair,
    land_twin,
    ahead_all,
    band_strip,
    load_sem,
    send_sem,
    recv_sem,
):
    leaves, size, count = leaf_source.shape
    r = lax.axis_index("prow")
    c = lax.axis_index("pcol")

    side = int(round(cols**0.5))
    chips = rows // 2

    def away(step, n):
        return min(step, n - step)

    col_steps = sorted(
        range(1, cols), key=lambda k: -away(k // side, side) - away(k % side, side)
    )
    row_steps = sorted(range(1, rows), key=lambda k: -away(k // 2, chips))
    col_peers = [
        (r, lax.rem(c // side + k // side, side) * side + lax.rem(c % side + k % side, side))
        for k in col_steps
    ]
    row_peers = [
        (lax.rem(r // 2 + k // 2, chips) * 2 + lax.rem(r % 2 + k % 2, 2), c) for k in row_steps
    ]
    along_cols = (1, c, col_peers)
    along_rows = (0, r, row_peers)
    twin = (r + 1 - 2 * (r % 2), c)
    along_chips = (0, r // 2, [peer for k, peer in zip(row_steps, row_peers) if k % 2 == 0])

    def whole(place):
        return stack.at[:, pl.ds(place * size, size), :]

    loads = [
        (leaf_source, source_in),
        (leaf_inverse, linv),
        (strip_inverse, sinv),
        (summit_strip, slift),
        (coupling, link),
        (summit_band, lift_in),
    ]
    for a in range(1, leaves):
        part = pl.ds(pair(a, 0), a)
        loads.append((leaf_blocks.at[part], lblk.at[part]))
    loads += [
        (band_blocks, whole(0)),
        (strip_blocks, whole(1)),
        (summit_blocks, whole(2)),
        (band_source, border_in.at[0]),
        (strip_source, border_in.at[1]),
        (summit_source, border_in.at[2]),
        (band_inverse, binv),
        (summit_inverse, uinv),
    ]
    copies = [
        pltpu.make_async_copy(src, dst, load_sem.at[place])
        for place, (src, dst) in enumerate(loads)
    ]
    for copy in copies:
        copy.start()

    barrier = pltpu.get_barrier_semaphore()
    for peer in col_peers + row_peers:
        pl.semaphore_signal(barrier, inc=1, device_id=peer, device_id_type=MESH)

    parent = [parents[b] for b in range(leaves)]
    reach = {}
    for a in range(leaves):
        for b in reversed(range(a)):
            met = (parent[b] == a).astype(jnp.int32)
            for k in range(b + 1, a):
                met = met + (parent[b] == k).astype(jnp.int32) * reach[a, k]
            reach[a, b] = met
    down = lax.broadcasted_iota(jnp.int32, (size, size), 0)
    across = lax.broadcasted_iota(jnp.int32, (size, size), 1)
    furthest = jnp.maximum(down, across)

    def prepare(a):
        linv[a] = jnp.where(furthest < widths[a], linv[a].astype(F32), 0.0).astype(BF16)
        now[a] = source_in[a].astype(F32).T.astype(BF16)
        for b in range(a):
            weight = reach[a, b].astype(F32)
            lblk[pair(a, b)] = (lblk[pair(a, b)].astype(F32) * weight).astype(BF16)

    used = []

    def ship(make_src, make_dst, peers, phase):
        @pl.when(c >= 0)
        def _():
            for peer in peers:
                pltpu.make_async_remote_copy(
                    src_ref=make_src(peer),
                    dst_ref=make_dst(peer),
                    send_sem=send_sem.at[phase],
                    recv_sem=recv_sem.at[phase],
                    device_id=peer,
                    device_id_type=MESH,
                ).start()

    def scatter(axis, phase, source, land):
        dim, me, peers = axis
        ship(lambda peer: source.at[peer[dim]], lambda peer: land.at[me], peers, phase)
        land[me] = source[me]
        used.append((peers, land, phase))

    def spread(axis, phase, value, land):
        dim, me, peers = axis
        land[me] = value
        ship(lambda peer: land.at[me], lambda peer: land.at[me], peers, phase)
        used.append((peers, land, phase))

    def bytes_of(peers, land, phase):
        part = land.at[pl.ds(0, len(peers))]
        return pltpu.make_async_remote_copy(
            src_ref=part,
            dst_ref=part,
            send_sem=send_sem.at[phase],
            recv_sem=recv_sem.at[phase],
            device_id=peers[0],
            device_id_type=MESH,
        )

    def meet(phase, source, land):
        pltpu.make_async_remote_copy(
            src_ref=source,
            dst_ref=land,
            send_sem=send_sem.at[phase],
            recv_sem=recv_sem.at[phase],
            device_id=twin,
            device_id_type=MESH,
        ).start()

    def gather(phase, source, land):
        copy = pltpu.make_async_remote_copy(
            src_ref=source,
            dst_ref=land,
            send_sem=send_sem.at[phase],
            recv_sem=recv_sem.at[phase],
            device_id=twin,
            device_id_type=MESH,
        )
        copy.wait_recv()
        copy.wait_send()

    def finish(axis, phase, land):
        bytes_of(axis[2], land, phase).wait_recv()

    def total(values):
        values = [values[k] for k in range(values.shape[0])]
        while len(values) > 1:
            values = [
                values[k] + values[k + 1] if k + 1 < len(values) else values[k]
                for k in range(0, len(values), 2)
            ]
        return values[0]

    def full(value):
        return value.reshape(count, size).astype(BF16)

    def parts(value, n):
        return value.reshape(n, count // n, size)

    def rounded(value):
        return value.astype(BF16).astype(F32)

    def build_bridge(i):
        below = nn(linv[2 * i + 1], lblk[pair(2 * i + 1, 2 * i)]).astype(BF16)
        bridge[i] = nn(below, linv[2 * i]).astype(BF16)

    def forward_step(i):
        rests = []
        for a in (2 * i, 2 * i + 1):
            rest = now[a].astype(F32)
            for b in range(2 * i):
                rest = rest - nt(solved[b], lblk[pair(a, b)])
            rests.append(rest.astype(BF16))
        solved[2 * i] = nt(rests[0], linv[2 * i]).astype(BF16)
        answer = nt(rests[1], linv[2 * i + 1]) - nt(rests[0], bridge[i])
        solved[2 * i + 1] = answer.astype(BF16)

    def backward_chain():
        for i in reversed(range(leaves // 2)):
            rests = []
            for a in (2 * i, 2 * i + 1):
                rest = solved[a].astype(F32)
                for b in range(2 * i + 2, leaves):
                    rest = rest - nn(solved[b], lblk[pair(b, a)])
                rests.append(rest.astype(BF16))
            answer = nn(rests[0], linv[2 * i]) - nn(rests[1], bridge[i])
            pend[2 * i] = answer
            solved[2 * i] = answer.astype(BF16)
            answer = nn(rests[1], linv[2 * i + 1])
            pend[2 * i + 1] = answer
            solved[2 * i + 1] = answer.astype(BF16)

    def term(values, blocks, place):
        part = pl.ds(place * size, size)
        result = nt(values[0], blocks[0, part, :])
        for a in range(1, leaves):
            result = result + nt(values[a], blocks[a, part, :])
        return result

    extra = 2 + 8 * PASSES
    slab = lift_in.shape[0]
    for copy in copies[:6]:
        copy.wait()
    prepare(0)
    copies[6].wait()
    prepare(1)
    build_bridge(0)
    for i in range(leaves // 2):
        if i + 1 < leaves // 2:
            for a in (2 * i + 2, 2 * i + 3):
                copies[5 + a].wait()
                prepare(a)
            build_bridge(i + 1)
        forward_step(i)
        if i == 0:
            lift[...] = jnp.zeros_like(lift)
            lift[pl.ds(pl.multiple_of(c * slab, slab), slab), :] = lift_in[...]
            turned = sinv[...].astype(F32).T.astype(BF16)
            lowered[...] = nn(turned, slift[...]).astype(BF16)
        if i == 1:
            turned = link[...].astype(F32).T.astype(BF16)
            ahead = nn(turned, lowered[...]) - lift[...].astype(F32)
            send_mat[...] = ahead.reshape(send_mat.shape)
            pl.semaphore_wait(barrier, rows + cols - 2)
            scatter(along_cols, extra, send_mat, land_mat.at[0])
    for copy in copies[leaves + 5 :]:
        copy.wait()
    sends[0] = parts(term(solved, stack, 0), cols)
    scatter(along_cols, 0, sends.at[0], lands.at[0])

    strip_term = term(solved, stack, 1)
    summit_term = term(solved, stack, 2)
    slabs[0] = parts(border_in[0].astype(F32).T, cols)
    slabs[1] = parts(border_in[1].astype(F32).T, rows)
    slabs[2] = parts(border_in[2].astype(F32).T, cols)
    band_src = slabs[0, c]
    strip_src = slabs[1, r]
    summit_src = slabs[2, c]
    strip_now = slabs[1].reshape(count, size)
    joined[...] = nn(sinv[...], link[...]).astype(BF16)

    def key_step(i):
        rests = []
        for a in (2 * i, 2 * i + 1):
            rest = stack[a].astype(F32)
            for b in range(2 * i + 2, leaves):
                rest = rest - nn(keys[b], lblk[pair(b, a)])
            rests.append(rest.astype(BF16))
        keys[2 * i] = (nn(rests[0], linv[2 * i]) - nn(rests[1], bridge[i])).astype(BF16)
        keys[2 * i + 1] = nn(rests[1], linv[2 * i + 1]).astype(BF16)

    pairs = leaves // 2
    key_step(pairs - 1)
    key_step(pairs - 2)
    finish(along_cols, 0, lands.at[0])
    rest = band_src - total(lands[0])
    band_slab = rounded(nt(rest.astype(BF16), binv[...]))
    spread(along_cols, 1, band_slab, lands.at[1])
    key_step(pairs - 3)
    finish(along_cols, 1, lands.at[1])
    band_all = full(lands[1])

    low = pl.ds(0, size)
    upper_rows = pl.ds(size, 2 * size)
    for p in range(PASSES):
        first = p == 0
        base = 2 + 8 * p
        pushed = strip_term + nt(band_all, link[...])
        sends[base] = parts(pushed, rows)
        scatter(along_rows, base, sends.at[base], lands.at[base])
        spare = (strip_now * (1.0 / rows) - pushed).astype(BF16)
        if not first:
            summit_term = term(now, keys, 2)
        raised = summit_term + nn(band_all, lift[...]) + nn(spare, lowered[...])
        sends[base + 1] = parts(raised, cols)
        scatter(along_cols, base + 1, sends.at[base + 1], lands.at[base + 1])
        if first:
            finish(along_cols, extra, land_mat.at[0])
            spread(along_cols, extra + 1, total(land_mat[0]), land_mat.at[1])
            for i in reversed(range(pairs - 3)):
                key_step(i)
            cross = nt(keys[0, low, :], keys[0])
            for a in range(1, leaves):
                cross = cross + nt(keys[a, low, :], keys[a])
            band_strip[...] = cross[:, size : 2 * size].astype(BF16)
            send_mats[:, 0] = cross[:, :size].reshape(cols, slab, size)
            product = nn(band_strip[...], lowered[...])
            send_mats[:, 1] = (product - cross[:, 2 * size :]).reshape(cols, slab, size)
            scatter(along_cols, extra + 2, send_mats, land_mats.at[0])
        else:
            for i in range(pairs):
                forward_step(i)
        finish(along_rows, base, lands.at[base])
        rest = strip_src - total(lands[base])
        strip_slab = rounded(nt(rest.astype(BF16), sinv[...]))
        spread(along_rows, base + 2, strip_slab, lands.at[base + 2])
        finish(along_cols, base + 1, lands.at[base + 1])
        own = total(lands[base + 1])
        land_twin[p, 0] = own
        meet(base + 3, land_twin.at[p, 0], land_twin.at[p, 1])
        backward_chain()
        if first:
            next_term = term(solved, keys, 0)
        gather(base + 3, land_twin.at[p, 0], land_twin.at[p, 1])
        spread(along_chips, base + 4, own + land_twin[p, 1], lands.at[base + 4])
        finish(along_rows, base + 2, lands.at[base + 2])
        strip_all = full(lands[base + 2])
        dropped = nn(strip_all, joined[...])
        strip_own = nn(strip_all, sinv[...])
        if first:
            send_pair[:, 0] = parts(dropped, cols)
            next_term = next_term - nt(strip_own.astype(BF16), band_strip[...])
            send_pair[:, 1] = parts(next_term, cols)
            scatter(along_cols, base + 5, send_pair, land_pair.at[0])
            finish(along_cols, extra + 2, land_mats.at[0])
            spread(along_cols, extra + 3, total(land_mats[0]), land_mats.at[1])
            finish(along_cols, extra + 1, land_mat.at[1])
            ahead_all[...] = land_mat[1].reshape(size, size).astype(BF16)
        else:
            sends[base + 5] = parts(dropped, cols)
            scatter(along_cols, base + 5, sends.at[base + 5], lands.at[base + 5])
        finish(along_chips, base + 4, lands.at[base + 4])
        rest = summit_src - total(lands[base + 4, : rows // 2])
        top = nt(rest.astype(BF16), uinv[...]).astype(BF16)
        top = nn(top, uinv[...]).astype(BF16)
        summit_src = top.astype(F32)
        spread(along_cols, base + 6, summit_src, lands.at[base + 6])
        back = nt(top, ahead_all[...])
        if first:
            finish(along_cols, base + 5, land_pair.at[0])
            sums = total(land_pair[0])
            rest = band_slab - sums[0] + back
            band_answer = rounded(nn(rest.astype(BF16), binv[...]))
            shift = nt(sums[1].astype(BF16), binv[...])
            spread(along_cols, base + 7, jnp.stack([band_answer, shift]), land_pair.at[1])
        else:
            finish(along_cols, base + 5, lands.at[base + 5])
            rest = band_slab - total(lands[base + 5]) + back
            band_answer = rounded(nn(rest.astype(BF16), binv[...]))
            spread(along_cols, base + 7, band_answer, lands.at[base + 7])
        finish(along_cols, base + 6, lands.at[base + 6])
        top_all = full(lands[base + 6])
        strip_answer = (strip_own - nt(top_all, lowered[...])).astype(BF16)
        strip_now = strip_answer.astype(F32)
        upper = jnp.concatenate([strip_answer, top_all], axis=1)
        for a in range(leaves):
            rest = pend[a] - nn(upper, keys[a, upper_rows, :])
            pend[a] = rest
            if first:
                now[a] = rest.astype(BF16)
        if first:
            slabs[1] = parts(strip_now, rows)
            strip_src = slabs[1, r]
            strip_term = term(now, keys, 1)
            finish(along_cols, extra + 3, land_mats.at[1])
            fold = land_mats[1, :, 0].reshape(size, size).astype(BF16)
            ahead_mat = binv[...].astype(F32) + nn(binv[...], fold)
            ahead_mat = ahead_mat.astype(BF16)
            fold = land_mats[1, :, 1].reshape(size, size).astype(BF16)
            lag = nn(binv[...], fold).astype(BF16)
            lagging = nt(top_all, lag)
            finish(along_cols, base + 7, land_pair.at[1])
            band_full = full(land_pair[1, :, 0])
            lagging = lagging + land_pair[1, :, 1].reshape(count, size)
            band_next = nt(band_full, ahead_mat) - lagging
            band_all = band_next.astype(BF16)
            band_place = rounded(band_next).reshape(cols, count // cols, size)
            slabs[0] = band_place
            band_slab = slabs[0, c]
            strip_term = strip_term - nn(band_full, band_strip[...])
        else:
            finish(along_cols, base + 7, lands.at[base + 7])
            band_full = full(lands[base + 7])
        for a in range(leaves):
            value = (pend[a] - nn(band_full, keys[a, low, :])).astype(BF16)
            if first:
                now[a] = value
            else:
                leaf_out[a] = value
    border_out[0] = band_full
    border_out[1] = strip_answer
    border_out[2] = top_all
    for peers, land, phase in used:
        bytes_of(peers, land, phase).wait_send()


def turn(leaf_in, border_in, leaf_out, band_out, strip_out, summit_out):
    for a in range(leaf_in.shape[0]):
        leaf_out[a] = leaf_in[a].astype(F32).T.astype(BF16)
    for place, out in enumerate((band_out, strip_out, summit_out)):
        out[...] = border_in[place].astype(F32).T.astype(BF16)


def per_device(
    rows,
    cols,
    leaf_source,
    band_source,
    strip_source,
    summit_source,
    leaf_inverse,
    band_inverse,
    strip_inverse,
    summit_inverse,
    leaf_blocks,
    band_blocks,
    strip_blocks,
    summit_blocks,
    coupling,
    summit_band,
    summit_strip,
    parents,
    widths,
):
    leaves, size, count = leaf_source.shape[2:]
    pairs = leaf_blocks.shape[2]
    slab = summit_band.shape[1]
    band_rhs = count // cols
    square = (size, size)
    anywhere = pl.BlockSpec(memory_space=pl.ANY)
    scalars = pl.BlockSpec(memory_space=pltpu.SMEM)
    vmem = pl.BlockSpec(memory_space=pltpu.VMEM)
    plain = pltpu.VMEM(square, BF16)
    phases = 6 + 8 * PASSES
    solved = pl.pallas_call(
        functools.partial(kernel, rows, cols),
        out_shape=(
            jax.ShapeDtypeStruct((leaves, count, size), BF16),
            jax.ShapeDtypeStruct((3, count, size), BF16),
        ),
        in_specs=[scalars] * 2 + [anywhere] * 15,
        out_specs=(vmem,) * 2,
        scratch_shapes=[
            pltpu.VMEM((leaves, size, count), BF16),
            pltpu.VMEM((3, size, count), BF16),
            pltpu.VMEM((leaves,) + square, BF16),
            pltpu.VMEM((pairs,) + square, BF16),
            pltpu.VMEM((leaves // 2,) + square, BF16),
            pltpu.VMEM((leaves, 3 * size, size), BF16),
            pltpu.VMEM((leaves, 3 * size, size), BF16),
            plain,
            plain,
            plain,
            plain,
            pltpu.VMEM((slab, size), BF16),
            plain,
            plain,
            plain,
            plain,
            pltpu.VMEM((leaves, count, size), BF16),
            pltpu.VMEM((leaves, count, size), BF16),
            pltpu.VMEM((leaves, count, size), F32),
            pltpu.VMEM((3, cols, band_rhs, size), F32),
            pltpu.VMEM((phases, cols, band_rhs, size), F32),
            pltpu.VMEM((cols, slab, size), F32),
            pltpu.VMEM((cols, 2, slab, size), F32),
            pltpu.VMEM((cols, 2, band_rhs, size), F32),
            pltpu.VMEM((phases, cols, band_rhs, size), F32),
            pltpu.VMEM((2, cols, slab, size), F32),
            pltpu.VMEM((2, cols, 2, slab, size), F32),
            pltpu.VMEM((2, cols, 2, band_rhs, size), F32),
            pltpu.VMEM((PASSES, 2, band_rhs, size), F32),
            plain,
            plain,
            pltpu.SemaphoreType.DMA((32,)),
            pltpu.SemaphoreType.DMA((phases,)),
            pltpu.SemaphoreType.DMA((phases,)),
        ],
        compiler_params=pltpu.CompilerParams(
            collective_id=0, has_side_effects=True, vmem_limit_bytes=56 * 1024 * 1024
        ),
        cost_estimate=pl.CostEstimate(
            flops=4_400_000_000, bytes_accessed=10_000_000, transcendentals=0
        ),
    )(
        parents[0, 0],
        widths[0, 0],
        leaf_source[0, 0],
        band_source[0],
        strip_source[0],
        summit_source,
        leaf_inverse[0, 0],
        band_inverse[0],
        strip_inverse[0],
        summit_inverse,
        leaf_blocks[0, 0],
        band_blocks[0, 0],
        strip_blocks[0, 0],
        summit_blocks[0, 0],
        coupling[0, 0],
        summit_band[0],
        summit_strip[0],
    )
    results = pl.pallas_call(
        turn,
        out_shape=(
            jax.ShapeDtypeStruct((leaves, size, count), BF16),
            jax.ShapeDtypeStruct((size, count), BF16),
            jax.ShapeDtypeStruct((size, count), BF16),
            jax.ShapeDtypeStruct((size, count), BF16),
        ),
        in_specs=[vmem] * 2,
        out_specs=(vmem,) * 4,
    )(*solved)
    return results[0][None, None], results[1][None], results[2][None], results[3]


def solution(mesh):
    placed = (
        P("prow", "pcol", None, None, None),
        P("prow", None, None),
        P("pcol", None, None),
        P(),
        P("prow", "pcol", None, None, None),
        P("prow", None, None),
        P("pcol", None, None),
        P(),
        P("prow", "pcol", None, None, None),
        P("prow", "pcol", None, None, None),
        P("prow", "pcol", None, None, None),
        P("prow", "pcol", None, None, None),
        P("prow", "pcol", None, None),
        P("prow", "pcol", None),
        P("pcol", None, None),
        P("prow", "pcol", None),
        P("prow", "pcol", None),
    )
    return jax.shard_map(
        functools.partial(per_device, mesh.shape["prow"], mesh.shape["pcol"]),
        mesh=mesh,
        in_specs=placed,
        out_specs=(
            P("prow", "pcol", None, None, None),
            P("prow", None, None),
            P("pcol", None, None),
            P(),
        ),
        check_vma=False,
    )
```

```python
import functools

import jax
import jax.numpy as jnp
from jax import lax
from jax.experimental import pallas as pl
from jax.experimental.pallas import tpu as pltpu
from jax.sharding import PartitionSpec as P

PASSES = 2
MESH = pl.DeviceIdType.MESH
F32 = jnp.float32
BF16 = jnp.bfloat16


def nn(left, right):
    return jnp.dot(left, right, preferred_element_type=F32)


def nt(left, right):
    return lax.dot_general(left, right, (((1,), (1,)), ((), ())), preferred_element_type=F32)


def pair(a, b):
    return a * (a - 1) // 2 + b


def kernel(
    rows,
    cols,
    parents,
    widths,
    leaf_source,
    band_source,
    strip_source,
    summit_source,
    leaf_inverse,
    band_inverse,
    strip_inverse,
    summit_inverse,
    leaf_blocks,
    band_blocks,
    strip_blocks,
    summit_blocks,
    coupling,
    summit_band,
    summit_strip,
    leaf_out,
    border_out,
    source_in,
    border_in,
    linv,
    lblk,
    bridge,
    stack,
    keys,
    link,
    binv,
    sinv,
    uinv,
    lift_in,
    lift,
    slift,
    lowered,
    joined,
    now,
    upright,
    solved,
    pend,
    slabs,
    sends,
    send_mat,
    send_mats,
    send_pair,
    lands,
    land_mat,
    land_mats,
    land_pair,
    land_twin,
    ahead_all,
    band_strip,
    load_sem,
    send_sem,
    recv_sem,
):
    leaves, size, count = leaf_source.shape
    r = lax.axis_index("prow")
    c = lax.axis_index("pcol")

    side = int(round(cols**0.5))
    chips = rows // 2

    def away(step, n):
        return min(step, n - step)

    col_steps = sorted(
        range(1, cols), key=lambda k: -away(k // side, side) - away(k % side, side)
    )
    row_steps = sorted(range(1, rows), key=lambda k: -away(k // 2, chips))
    col_peers = [
        (r, lax.rem(c // side + k // side, side) * side + lax.rem(c % side + k % side, side))
        for k in col_steps
    ]
    row_peers = [
        (lax.rem(r // 2 + k // 2, chips) * 2 + lax.rem(r % 2 + k % 2, 2), c) for k in row_steps
    ]
    along_cols = (1, c, col_peers)
    along_rows = (0, r, row_peers)
    twin = (r + 1 - 2 * (r % 2), c)
    along_chips = (0, r // 2, [peer for k, peer in zip(row_steps, row_peers) if k % 2 == 0])

    def whole(place):
        return stack.at[:, pl.ds(place * size, size), :]

    loads = [
        (leaf_source, source_in),
        (leaf_inverse, linv),
    ]
    for a in range(1, leaves):
        part = pl.ds(pair(a, 0), a)
        loads.append((leaf_blocks.at[part], lblk.at[part]))
    loads += [
        (band_blocks, whole(0)),
        (strip_inverse, sinv),
        (summit_strip, slift),
        (coupling, link),
        (summit_band, lift_in),
        (strip_blocks, whole(1)),
        (summit_blocks, whole(2)),
        (band_source, border_in.at[0]),
        (strip_source, border_in.at[1]),
        (summit_source, border_in.at[2]),
        (band_inverse, binv),
        (summit_inverse, uinv),
    ]
    copies = [
        pltpu.make_async_copy(src, dst, load_sem.at[place])
        for place, (src, dst) in enumerate(loads)
    ]
    soon = leaves + 2
    for copy in copies[:soon]:
        copy.start()

    barrier = pltpu.get_barrier_semaphore()
    for peer in col_peers + row_peers:
        pl.semaphore_signal(barrier, inc=1, device_id=peer, device_id_type=MESH)

    parent = [parents[b] for b in range(leaves)]
    reach = {}
    for a in range(leaves):
        for b in reversed(range(a)):
            met = (parent[b] == a).astype(jnp.int32)
            for k in range(b + 1, a):
                met = met + (parent[b] == k).astype(jnp.int32) * reach[a, k]
            reach[a, b] = met
    down = lax.broadcasted_iota(jnp.int32, (size, size), 0)
    across = lax.broadcasted_iota(jnp.int32, (size, size), 1)
    furthest = jnp.maximum(down, across)

    def prepare(a):
        linv[a] = jnp.where(furthest < widths[a], linv[a].astype(F32), 0.0).astype(BF16)
        for b in range(a):
            weight = reach[a, b].astype(F32)
            lblk[pair(a, b)] = (lblk[pair(a, b)].astype(F32) * weight).astype(BF16)

    used = []

    def ship(make_src, make_dst, peers, phase):
        @pl.when(c >= 0)
        def _():
            for peer in peers:
                pltpu.make_async_remote_copy(
                    src_ref=make_src(peer),
                    dst_ref=make_dst(peer),
                    send_sem=send_sem.at[phase],
                    recv_sem=recv_sem.at[phase],
                    device_id=peer,
                    device_id_type=MESH,
                ).start()

    def scatter(axis, phase, source, land):
        dim, me, peers = axis
        ship(lambda peer: source.at[peer[dim]], lambda peer: land.at[me], peers, phase)
        land[me] = source[me]
        used.append((peers, land, phase))

    def spread(axis, phase, value, land):
        dim, me, peers = axis
        land[me] = value
        ship(lambda peer: land.at[me], lambda peer: land.at[me], peers, phase)
        used.append((peers, land, phase))

    def bytes_of(peers, land, phase):
        part = land.at[pl.ds(0, len(peers))]
        return pltpu.make_async_remote_copy(
            src_ref=part,
            dst_ref=part,
            send_sem=send_sem.at[phase],
            recv_sem=recv_sem.at[phase],
            device_id=peers[0],
            device_id_type=MESH,
        )

    def meet(phase, source, land):
        pltpu.make_async_remote_copy(
            src_ref=source,
            dst_ref=land,
            send_sem=send_sem.at[phase],
            recv_sem=recv_sem.at[phase],
            device_id=twin,
            device_id_type=MESH,
        ).start()

    def gather(phase, source, land):
        copy = pltpu.make_async_remote_copy(
            src_ref=source,
            dst_ref=land,
            send_sem=send_sem.at[phase],
            recv_sem=recv_sem.at[phase],
            device_id=twin,
            device_id_type=MESH,
        )
        copy.wait_recv()
        copy.wait_send()

    def finish(axis, phase, land):
        bytes_of(axis[2], land, phase).wait_recv()

    def total(values):
        values = [values[k] for k in range(values.shape[0])]
        while len(values) > 1:
            values = [
                values[k] + values[k + 1] if k + 1 < len(values) else values[k]
                for k in range(0, len(values), 2)
            ]
        return values[0]

    def full(value):
        return value.reshape(count, size).astype(BF16)

    def parts(value, n):
        return value.reshape(n, count // n, size)

    def rounded(value):
        return value.astype(BF16).astype(F32)

    def build_bridge(i):
        below = nn(linv[2 * i + 1], lblk[pair(2 * i + 1, 2 * i)]).astype(BF16)
        bridge[i] = nn(below, linv[2 * i]).astype(BF16)

    def forward_step(i):
        rests = []
        for a in (2 * i, 2 * i + 1):
            rest = now[a].astype(F32)
            for b in range(2 * i):
                rest = rest - nt(solved[b], lblk[pair(a, b)])
            rests.append(rest.astype(BF16))
        solved[2 * i] = nt(rests[0], linv[2 * i]).astype(BF16)
        answer = nt(rests[1], linv[2 * i + 1]) - nt(rests[0], bridge[i])
        solved[2 * i + 1] = answer.astype(BF16)

    def first_step(i):
        rests = []
        for a in (2 * i, 2 * i + 1):
            rest = source_in[a].astype(F32)
            for b in range(2 * i):
                rest = rest - nn(lblk[pair(a, b)], upright[b])
            rests.append(rest.astype(BF16))
        upright[2 * i] = nn(linv[2 * i], rests[0]).astype(BF16)
        answer = nn(linv[2 * i + 1], rests[1]) - nn(bridge[i], rests[0])
        upright[2 * i + 1] = answer.astype(BF16)

    def backward_chain():
        for i in reversed(range(leaves // 2)):
            rests = []
            for a in (2 * i, 2 * i + 1):
                rest = solved[a].astype(F32)
                for b in range(2 * i + 2, leaves):
                    rest = rest - nn(solved[b], lblk[pair(b, a)])
                rests.append(rest.astype(BF16))
            answer = nn(rests[0], linv[2 * i]) - nn(rests[1], bridge[i])
            pend[2 * i] = answer
            solved[2 * i] = answer.astype(BF16)
            answer = nn(rests[1], linv[2 * i + 1])
            pend[2 * i + 1] = answer
            solved[2 * i + 1] = answer.astype(BF16)

    def term(values, blocks, place):
        part = pl.ds(place * size, size)
        result = nt(values[0], blocks[0, part, :])
        for a in range(1, leaves):
            result = result + nt(values[a], blocks[a, part, :])
        return result

    extra = 2 + 8 * PASSES
    slab = lift_in.shape[0]
    for copy in copies[:2]:
        copy.wait()
    prepare(0)
    copies[2].wait()
    prepare(1)
    build_bridge(0)
    for i in range(leaves // 2):
        if i + 1 < leaves // 2:
            for a in (2 * i + 2, 2 * i + 3):
                copies[1 + a].wait()
                prepare(a)
            build_bridge(i + 1)
        first_step(i)
        if i == leaves // 2 - 2:
            for copy in copies[soon:]:
                copy.start()
    copies[soon - 1].wait()
    start_term = nn(stack[0, pl.ds(0, size), :], upright[0])
    for a in range(1, leaves):
        start_term = start_term + nn(stack[a, pl.ds(0, size), :], upright[a])
    sends[0] = parts(start_term.T, cols)
    pl.semaphore_wait(barrier, rows + cols - 2)
    scatter(along_cols, 0, sends.at[0], lands.at[0])
    for copy in copies[soon:]:
        copy.wait()
    lift[...] = jnp.zeros_like(lift)
    lift[pl.ds(pl.multiple_of(c * slab, slab), slab), :] = lift_in[...]
    turned = sinv[...].astype(F32).T.astype(BF16)
    lowered[...] = nn(turned, slift[...]).astype(BF16)
    turned = link[...].astype(F32).T.astype(BF16)
    ahead = nn(turned, lowered[...]) - lift[...].astype(F32)
    send_mat[...] = ahead.reshape(send_mat.shape)

    for a in range(leaves):
        solved[a] = upright[a].astype(F32).T.astype(BF16)
    strip_term = term(solved, stack, 1)
    summit_term = term(solved, stack, 2)
    slabs[0] = parts(border_in[0].astype(F32).T, cols)
    slabs[1] = parts(border_in[1].astype(F32).T, rows)
    slabs[2] = parts(border_in[2].astype(F32).T, cols)
    band_src = slabs[0, c]
    strip_src = slabs[1, r]
    summit_src = slabs[2, c]
    strip_now = slabs[1].reshape(count, size)
    joined[...] = nn(sinv[...], link[...]).astype(BF16)

    def key_step(i):
        rests = []
        for a in (2 * i, 2 * i + 1):
            rest = stack[a].astype(F32)
            for b in range(2 * i + 2, leaves):
                rest = rest - nn(keys[b], lblk[pair(b, a)])
            rests.append(rest.astype(BF16))
        keys[2 * i] = (nn(rests[0], linv[2 * i]) - nn(rests[1], bridge[i])).astype(BF16)
        keys[2 * i + 1] = nn(rests[1], linv[2 * i + 1]).astype(BF16)

    pairs = leaves // 2
    key_step(pairs - 1)
    key_step(pairs - 2)
    finish(along_cols, 0, lands.at[0])
    rest = band_src - total(lands[0])
    band_slab = rounded(nt(rest.astype(BF16), binv[...]))
    spread(along_cols, 1, band_slab, lands.at[1])
    scatter(along_cols, extra, send_mat, land_mat.at[0])
    for i in reversed(range(pairs - 2)):
        key_step(i)
    finish(along_cols, 1, lands.at[1])
    band_all = full(lands[1])

    low = pl.ds(0, size)
    upper_rows = pl.ds(size, 2 * size)
    for p in range(PASSES):
        first = p == 0
        base = 2 + 8 * p
        pushed = strip_term + nt(band_all, link[...])
        sends[base] = parts(pushed, rows)
        scatter(along_rows, base, sends.at[base], lands.at[base])
        spare = (strip_now * (1.0 / rows) - pushed).astype(BF16)
        if not first:
            summit_term = term(now, keys, 2)
        raised = summit_term + nn(band_all, lift[...]) + nn(spare, lowered[...])
        sends[base + 1] = parts(raised, cols)
        scatter(along_cols, base + 1, sends.at[base + 1], lands.at[base + 1])
        if first:
            finish(along_cols, extra, land_mat.at[0])
            spread(along_cols, extra + 1, total(land_mat[0]), land_mat.at[1])
            cross = nt(keys[0, low, :], keys[0])
            for a in range(1, leaves):
                cross = cross + nt(keys[a, low, :], keys[a])
            band_strip[...] = cross[:, size : 2 * size].astype(BF16)
            send_mats[:, 0] = cross[:, :size].reshape(cols, slab, size)
            product = nn(band_strip[...], lowered[...])
            send_mats[:, 1] = (product - cross[:, 2 * size :]).reshape(cols, slab, size)
            scatter(along_cols, extra + 2, send_mats, land_mats.at[0])
        else:
            for i in range(pairs):
                forward_step(i)
        finish(along_rows, base, lands.at[base])
        rest = strip_src - total(lands[base])
        strip_slab = rounded(nt(rest.astype(BF16), sinv[...]))
        spread(along_rows, base + 2, strip_slab, lands.at[base + 2])
        finish(along_cols, base + 1, lands.at[base + 1])
        own = total(lands[base + 1])
        land_twin[p, 0] = own
        meet(base + 3, land_twin.at[p, 0], land_twin.at[p, 1])
        backward_chain()
        if first:
            next_term = term(solved, keys, 0)
        gather(base + 3, land_twin.at[p, 0], land_twin.at[p, 1])
        spread(along_chips, base + 4, own + land_twin[p, 1], lands.at[base + 4])
        finish(along_rows, base + 2, lands.at[base + 2])
        strip_all = full(lands[base + 2])
        dropped = nn(strip_all, joined[...])
        strip_own = nn(strip_all, sinv[...])
        if first:
            send_pair[:, 0] = parts(dropped, cols)
            next_term = next_term - nt(strip_own.astype(BF16), band_strip[...])
            send_pair[:, 1] = parts(next_term, cols)
            scatter(along_cols, base + 5, send_pair, land_pair.at[0])
            finish(along_cols, extra + 2, land_mats.at[0])
            spread(along_cols, extra + 3, total(land_mats[0]), land_mats.at[1])
            finish(along_cols, extra + 1, land_mat.at[1])
            ahead_all[...] = land_mat[1].reshape(size, size).astype(BF16)
        else:
            sends[base + 5] = parts(dropped, cols)
            scatter(along_cols, base + 5, sends.at[base + 5], lands.at[base + 5])
        finish(along_chips, base + 4, lands.at[base + 4])
        rest = summit_src - total(lands[base + 4, : rows // 2])
        top = nt(rest.astype(BF16), uinv[...]).astype(BF16)
        top = nn(top, uinv[...]).astype(BF16)
        summit_src = top.astype(F32)
        spread(along_cols, base + 6, summit_src, lands.at[base + 6])
        back = nt(top, ahead_all[...])
        if first:
            finish(along_cols, base + 5, land_pair.at[0])
            sums = total(land_pair[0])
            rest = band_slab - sums[0] + back
            band_answer = rounded(nn(rest.astype(BF16), binv[...]))
            shift = nt(sums[1].astype(BF16), binv[...])
            spread(along_cols, base + 7, jnp.stack([band_answer, shift]), land_pair.at[1])
        else:
            finish(along_cols, base + 5, lands.at[base + 5])
            rest = band_slab - total(lands[base + 5]) + back
            band_answer = rounded(nn(rest.astype(BF16), binv[...]))
            spread(along_cols, base + 7, band_answer, lands.at[base + 7])
        finish(along_cols, base + 6, lands.at[base + 6])
        top_all = full(lands[base + 6])
        strip_answer = (strip_own - nt(top_all, lowered[...])).astype(BF16)
        strip_now = strip_answer.astype(F32)
        upper = jnp.concatenate([strip_answer, top_all], axis=1)
        for a in range(leaves):
            rest = pend[a] - nn(upper, keys[a, upper_rows, :])
            pend[a] = rest
            if first:
                now[a] = rest.astype(BF16)
        if first:
            slabs[1] = parts(strip_now, rows)
            strip_src = slabs[1, r]
            strip_term = term(now, keys, 1)
            finish(along_cols, extra + 3, land_mats.at[1])
            fold = land_mats[1, :, 0].reshape(size, size).astype(BF16)
            ahead_mat = binv[...].astype(F32) + nn(binv[...], fold)
            ahead_mat = ahead_mat.astype(BF16)
            fold = land_mats[1, :, 1].reshape(size, size).astype(BF16)
            lag = nn(binv[...], fold).astype(BF16)
            lagging = nt(top_all, lag)
            finish(along_cols, base + 7, land_pair.at[1])
            band_full = full(land_pair[1, :, 0])
            lagging = lagging + land_pair[1, :, 1].reshape(count, size)
            band_next = nt(band_full, ahead_mat) - lagging
            band_all = band_next.astype(BF16)
            band_place = rounded(band_next).reshape(cols, count // cols, size)
            slabs[0] = band_place
            band_slab = slabs[0, c]
            strip_term = strip_term - nn(band_full, band_strip[...])
        else:
            finish(along_cols, base + 7, lands.at[base + 7])
            band_full = full(lands[base + 7])
        for a in range(leaves):
            value = (pend[a] - nn(band_full, keys[a, low, :])).astype(BF16)
            if first:
                now[a] = value
            else:
                leaf_out[a] = value
    border_out[0] = band_full
    border_out[1] = strip_answer
    border_out[2] = top_all
    for peers, land, phase in used:
        bytes_of(peers, land, phase).wait_send()


def turn(leaf_in, border_in, leaf_out, band_out, strip_out, summit_out):
    for a in range(leaf_in.shape[0]):
        leaf_out[a] = leaf_in[a].astype(F32).T.astype(BF16)
    for place, out in enumerate((band_out, strip_out, summit_out)):
        out[...] = border_in[place].astype(F32).T.astype(BF16)


def per_device(
    rows,
    cols,
    leaf_source,
    band_source,
    strip_source,
    summit_source,
    leaf_inverse,
    band_inverse,
    strip_inverse,
    summit_inverse,
    leaf_blocks,
    band_blocks,
    strip_blocks,
    summit_blocks,
    coupling,
    summit_band,
    summit_strip,
    parents,
    widths,
):
    leaves, size, count = leaf_source.shape[2:]
    pairs = leaf_blocks.shape[2]
    slab = summit_band.shape[1]
    band_rhs = count // cols
    square = (size, size)
    anywhere = pl.BlockSpec(memory_space=pl.ANY)
    scalars = pl.BlockSpec(memory_space=pltpu.SMEM)
    vmem = pl.BlockSpec(memory_space=pltpu.VMEM)
    plain = pltpu.VMEM(square, BF16)
    phases = 6 + 8 * PASSES
    solved = pl.pallas_call(
        functools.partial(kernel, rows, cols),
        out_shape=(
            jax.ShapeDtypeStruct((leaves, count, size), BF16),
            jax.ShapeDtypeStruct((3, count, size), BF16),
        ),
        in_specs=[scalars] * 2 + [anywhere] * 15,
        out_specs=(vmem,) * 2,
        scratch_shapes=[
            pltpu.VMEM((leaves, size, count), BF16),
            pltpu.VMEM((3, size, count), BF16),
            pltpu.VMEM((leaves,) + square, BF16),
            pltpu.VMEM((pairs,) + square, BF16),
            pltpu.VMEM((leaves // 2,) + square, BF16),
            pltpu.VMEM((leaves, 3 * size, size), BF16),
            pltpu.VMEM((leaves, 3 * size, size), BF16),
            plain,
            plain,
            plain,
            plain,
            pltpu.VMEM((slab, size), BF16),
            plain,
            plain,
            plain,
            plain,
            pltpu.VMEM((leaves, count, size), BF16),
            pltpu.VMEM((leaves, size, count), BF16),
            pltpu.VMEM((leaves, count, size), BF16),
            pltpu.VMEM((leaves, count, size), F32),
            pltpu.VMEM((3, cols, band_rhs, size), F32),
            pltpu.VMEM((phases, cols, band_rhs, size), F32),
            pltpu.VMEM((cols, slab, size), F32),
            pltpu.VMEM((cols, 2, slab, size), F32),
            pltpu.VMEM((cols, 2, band_rhs, size), F32),
            pltpu.VMEM((phases, cols, band_rhs, size), F32),
            pltpu.VMEM((2, cols, slab, size), F32),
            pltpu.VMEM((2, cols, 2, slab, size), F32),
            pltpu.VMEM((2, cols, 2, band_rhs, size), F32),
            pltpu.VMEM((PASSES, 2, band_rhs, size), F32),
            plain,
            plain,
            pltpu.SemaphoreType.DMA((32,)),
            pltpu.SemaphoreType.DMA((phases,)),
            pltpu.SemaphoreType.DMA((phases,)),
        ],
        compiler_params=pltpu.CompilerParams(
            collective_id=0, has_side_effects=True, vmem_limit_bytes=56 * 1024 * 1024
        ),
        cost_estimate=pl.CostEstimate(
            flops=4_400_000_000, bytes_accessed=10_000_000, transcendentals=0
        ),
    )(
        parents[0, 0],
        widths[0, 0],
        leaf_source[0, 0],
        band_source[0],
        strip_source[0],
        summit_source,
        leaf_inverse[0, 0],
        band_inverse[0],
        strip_inverse[0],
        summit_inverse,
        leaf_blocks[0, 0],
        band_blocks[0, 0],
        strip_blocks[0, 0],
        summit_blocks[0, 0],
        coupling[0, 0],
        summit_band[0],
        summit_strip[0],
    )
    results = pl.pallas_call(
        turn,
        out_shape=(
            jax.ShapeDtypeStruct((leaves, size, count), BF16),
            jax.ShapeDtypeStruct((size, count), BF16),
            jax.ShapeDtypeStruct((size, count), BF16),
            jax.ShapeDtypeStruct((size, count), BF16),
        ),
        in_specs=[vmem] * 2,
        out_specs=(vmem,) * 4,
    )(*solved)
    return results[0][None, None], results[1][None], results[2][None], results[3]


def solution(mesh):
    placed = (
        P("prow", "pcol", None, None, None),
        P("prow", None, None),
        P("pcol", None, None),
        P(),
        P("prow", "pcol", None, None, None),
        P("prow", None, None),
        P("pcol", None, None),
        P(),
        P("prow", "pcol", None, None, None),
        P("prow", "pcol", None, None, None),
        P("prow", "pcol", None, None, None),
        P("prow", "pcol", None, None, None),
        P("prow", "pcol", None, None),
        P("prow", "pcol", None),
        P("pcol", None, None),
        P("prow", "pcol", None),
        P("prow", "pcol", None),
    )
    return jax.shard_map(
        functools.partial(per_device, mesh.shape["prow"], mesh.shape["pcol"]),
        mesh=mesh,
        in_specs=placed,
        out_specs=(
            P("prow", "pcol", None, None, None),
            P("prow", None, None),
            P("pcol", None, None),
            P(),
        ),
        check_vma=False,
    )
```

```python
import functools

import jax
import jax.numpy as jnp
from jax import lax
from jax.experimental import pallas as pl
from jax.experimental.pallas import tpu as pltpu
from jax.sharding import PartitionSpec as P

PASSES = 2
MESH = pl.DeviceIdType.MESH
F32 = jnp.float32
BF16 = jnp.bfloat16


def nn(left, right):
    return jnp.dot(left, right, preferred_element_type=F32)


def nt(left, right):
    return lax.dot_general(left, right, (((1,), (1,)), ((), ())), preferred_element_type=F32)


def pair(a, b):
    return a * (a - 1) // 2 + b


def kernel(
    rows,
    cols,
    parents,
    widths,
    leaf_source,
    band_source,
    strip_source,
    summit_source,
    leaf_inverse,
    band_inverse,
    strip_inverse,
    summit_inverse,
    leaf_blocks,
    band_blocks,
    strip_blocks,
    summit_blocks,
    coupling,
    summit_band,
    summit_strip,
    leaf_out,
    border_out,
    source_in,
    border_in,
    linv,
    lblk,
    bridge,
    stack,
    keys,
    link,
    binv,
    sinv,
    uinv,
    lift_in,
    lift,
    slift,
    lowered,
    joined,
    now,
    upright,
    solved,
    pend,
    slabs,
    sends,
    send_mat,
    send_mats,
    send_pair,
    lands,
    land_mat,
    land_mats,
    land_pair,
    land_twin,
    ahead_all,
    band_strip,
    load_sem,
    send_sem,
    recv_sem,
):
    leaves, size, count = leaf_source.shape
    r = lax.axis_index("prow")
    c = lax.axis_index("pcol")

    side = int(round(cols**0.5))
    chips = rows // 2

    def away(step, n):
        return min(step, n - step)

    col_steps = sorted(
        range(1, cols), key=lambda k: -away(k // side, side) - away(k % side, side)
    )
    row_steps = sorted(range(1, rows), key=lambda k: -away(k // 2, chips))
    col_peers = [
        (r, lax.rem(c // side + k // side, side) * side + lax.rem(c % side + k % side, side))
        for k in col_steps
    ]
    row_peers = [
        (lax.rem(r // 2 + k // 2, chips) * 2 + lax.rem(r % 2 + k % 2, 2), c) for k in row_steps
    ]
    along_cols = (1, c, col_peers)
    along_rows = (0, r, row_peers)
    twin = (r + 1 - 2 * (r % 2), c)
    along_chips = (0, r // 2, [peer for k, peer in zip(row_steps, row_peers) if k % 2 == 0])

    def whole(place):
        return stack.at[:, pl.ds(place * size, size), :]

    loads = [
        (leaf_source, source_in),
        (leaf_inverse, linv),
    ]
    for a in range(1, leaves):
        part = pl.ds(pair(a, 0), a)
        loads.append((leaf_blocks.at[part], lblk.at[part]))
    loads += [
        (band_blocks, whole(0)),
        (strip_inverse, sinv),
        (summit_strip, slift),
        (coupling, link),
        (summit_band, lift_in),
        (strip_blocks, whole(1)),
        (summit_blocks, whole(2)),
        (band_source, border_in.at[0]),
        (strip_source, border_in.at[1]),
        (summit_source, border_in.at[2]),
        (band_inverse, binv),
        (summit_inverse, uinv),
    ]
    copies = [
        pltpu.make_async_copy(src, dst, load_sem.at[place])
        for place, (src, dst) in enumerate(loads)
    ]
    soon = leaves + 2
    for copy in copies[:soon]:
        copy.start()

    barrier = pltpu.get_barrier_semaphore()
    for peer in col_peers + row_peers:
        pl.semaphore_signal(barrier, inc=1, device_id=peer, device_id_type=MESH)

    parent = [parents[b] for b in range(leaves)]
    reach = {}
    for a in range(leaves):
        for b in reversed(range(a)):
            met = (parent[b] == a).astype(jnp.int32)
            for k in range(b + 1, a):
                met = met + (parent[b] == k).astype(jnp.int32) * reach[a, k]
            reach[a, b] = met
    down = lax.broadcasted_iota(jnp.int32, (size, size), 0)
    across = lax.broadcasted_iota(jnp.int32, (size, size), 1)
    furthest = jnp.maximum(down, across)

    def prepare(a):
        linv[a] = jnp.where(furthest < widths[a], linv[a].astype(F32), 0.0).astype(BF16)
        for b in range(a):
            weight = reach[a, b].astype(F32)
            lblk[pair(a, b)] = (lblk[pair(a, b)].astype(F32) * weight).astype(BF16)

    used = []

    def ship(make_src, make_dst, peers, phase):
        @pl.when(c >= 0)
        def _():
            for peer in peers:
                pltpu.make_async_remote_copy(
                    src_ref=make_src(peer),
                    dst_ref=make_dst(peer),
                    send_sem=send_sem.at[phase],
                    recv_sem=recv_sem.at[phase],
                    device_id=peer,
                    device_id_type=MESH,
                ).start()

    def scatter(axis, phase, source, land):
        dim, me, peers = axis
        ship(lambda peer: source.at[peer[dim]], lambda peer: land.at[me], peers, phase)
        land[me] = source[me]
        used.append((peers, land, phase))

    def spread(axis, phase, value, land):
        dim, me, peers = axis
        land[me] = value
        ship(lambda peer: land.at[me], lambda peer: land.at[me], peers, phase)
        used.append((peers, land, phase))

    def bytes_of(peers, land, phase):
        part = land.at[pl.ds(0, len(peers))]
        return pltpu.make_async_remote_copy(
            src_ref=part,
            dst_ref=part,
            send_sem=send_sem.at[phase],
            recv_sem=recv_sem.at[phase],
            device_id=peers[0],
            device_id_type=MESH,
        )

    def meet(phase, source, land):
        pltpu.make_async_remote_copy(
            src_ref=source,
            dst_ref=land,
            send_sem=send_sem.at[phase],
            recv_sem=recv_sem.at[phase],
            device_id=twin,
            device_id_type=MESH,
        ).start()

    def gather(phase, source, land):
        copy = pltpu.make_async_remote_copy(
            src_ref=source,
            dst_ref=land,
            send_sem=send_sem.at[phase],
            recv_sem=recv_sem.at[phase],
            device_id=twin,
            device_id_type=MESH,
        )
        copy.wait_recv()
        copy.wait_send()

    def finish(axis, phase, land):
        bytes_of(axis[2], land, phase).wait_recv()

    def total(values):
        values = [values[k] for k in range(values.shape[0])]
        while len(values) > 1:
            values = [
                values[k] + values[k + 1] if k + 1 < len(values) else values[k]
                for k in range(0, len(values), 2)
            ]
        return values[0]

    def full(value):
        return value.reshape(count, size).astype(BF16)

    def parts(value, n):
        return value.reshape(n, count // n, size)

    def rounded(value):
        return value.astype(BF16).astype(F32)

    def build_bridge(i):
        below = nn(linv[2 * i + 1], lblk[pair(2 * i + 1, 2 * i)]).astype(BF16)
        bridge[i] = nn(below, linv[2 * i]).astype(BF16)

    def forward_step(i):
        rests = []
        for a in (2 * i, 2 * i + 1):
            rest = now[a].astype(F32)
            for b in range(2 * i):
                rest = rest - nt(solved[b], lblk[pair(a, b)])
            rests.append(rest.astype(BF16))
        solved[2 * i] = nt(rests[0], linv[2 * i]).astype(BF16)
        answer = nt(rests[1], linv[2 * i + 1]) - nt(rests[0], bridge[i])
        solved[2 * i + 1] = answer.astype(BF16)

    def first_step(i):
        rests = []
        for a in (2 * i, 2 * i + 1):
            rest = source_in[a].astype(F32)
            for b in range(2 * i):
                rest = rest - nn(lblk[pair(a, b)], upright[b])
            rests.append(rest.astype(BF16))
        upright[2 * i] = nn(linv[2 * i], rests[0]).astype(BF16)
        answer = nn(linv[2 * i + 1], rests[1]) - nn(bridge[i], rests[0])
        upright[2 * i + 1] = answer.astype(BF16)

    def backward_chain():
        for i in reversed(range(leaves // 2)):
            rests = []
            for a in (2 * i, 2 * i + 1):
                rest = solved[a].astype(F32)
                for b in range(2 * i + 2, leaves):
                    rest = rest - nn(solved[b], lblk[pair(b, a)])
                rests.append(rest.astype(BF16))
            answer = nn(rests[0], linv[2 * i]) - nn(rests[1], bridge[i])
            pend[2 * i] = answer
            solved[2 * i] = answer.astype(BF16)
            answer = nn(rests[1], linv[2 * i + 1])
            pend[2 * i + 1] = answer
            solved[2 * i + 1] = answer.astype(BF16)

    def term(values, blocks, place):
        part = pl.ds(place * size, size)
        result = nt(values[0], blocks[0, part, :])
        for a in range(1, leaves):
            result = result + nt(values[a], blocks[a, part, :])
        return result

    extra = 2 + 8 * PASSES
    slab = lift_in.shape[0]
    for copy in copies[:2]:
        copy.wait()
    prepare(0)
    copies[2].wait()
    prepare(1)
    build_bridge(0)
    for i in range(leaves // 2):
        if i + 1 < leaves // 2:
            for a in (2 * i + 2, 2 * i + 3):
                copies[1 + a].wait()
                prepare(a)
            build_bridge(i + 1)
        first_step(i)
        if i == leaves // 2 - 2:
            for copy in copies[soon:]:
                copy.start()
    copies[soon - 1].wait()
    start_term = nn(stack[0, pl.ds(0, size), :], upright[0])
    for a in range(1, leaves):
        start_term = start_term + nn(stack[a, pl.ds(0, size), :], upright[a])
    sends[0] = parts(start_term.T, cols)
    pl.semaphore_wait(barrier, rows + cols - 2)
    scatter(along_cols, 0, sends.at[0], lands.at[0])
    for copy in copies[soon:]:
        copy.wait()
    lift[...] = jnp.zeros_like(lift)
    lift[pl.ds(pl.multiple_of(c * slab, slab), slab), :] = lift_in[...]
    turned = sinv[...].astype(F32).T.astype(BF16)
    lowered[...] = nn(turned, slift[...]).astype(BF16)
    turned = link[...].astype(F32).T.astype(BF16)
    ahead = nn(turned, lowered[...]) - lift[...].astype(F32)
    send_mat[...] = ahead.reshape(send_mat.shape)

    for a in range(leaves):
        solved[a] = upright[a].astype(F32).T.astype(BF16)
    strip_term = term(solved, stack, 1)
    summit_term = term(solved, stack, 2)
    slabs[0] = parts(border_in[0].astype(F32).T, cols)
    slabs[1] = parts(border_in[1].astype(F32).T, rows)
    slabs[2] = parts(border_in[2].astype(F32).T, cols)
    band_src = slabs[0, c]
    strip_src = slabs[1, r]
    summit_src = slabs[2, c]
    strip_now = slabs[1].reshape(count, size)
    joined[...] = nn(sinv[...], link[...]).astype(BF16)

    def key_step(i):
        rests = []
        for a in (2 * i, 2 * i + 1):
            rest = stack[a].astype(F32)
            for b in range(2 * i + 2, leaves):
                rest = rest - nn(keys[b], lblk[pair(b, a)])
            rests.append(rest.astype(BF16))
        keys[2 * i] = (nn(rests[0], linv[2 * i]) - nn(rests[1], bridge[i])).astype(BF16)
        keys[2 * i + 1] = nn(rests[1], linv[2 * i + 1]).astype(BF16)

    pairs = leaves // 2
    key_step(pairs - 1)
    key_step(pairs - 2)
    key_step(pairs - 3)
    finish(along_cols, 0, lands.at[0])
    rest = band_src - total(lands[0])
    band_slab = rounded(nt(rest.astype(BF16), binv[...]))
    spread(along_cols, 1, band_slab, lands.at[1])
    scatter(along_cols, extra, send_mat, land_mat.at[0])
    for i in reversed(range(pairs - 3)):
        key_step(i)
    low = pl.ds(0, size)
    cross = nt(keys[0, low, :], keys[0])
    for a in range(1, leaves):
        cross = cross + nt(keys[a, low, :], keys[a])
    band_strip[...] = cross[:, size : 2 * size].astype(BF16)
    send_mats[:, 0] = cross[:, :size].reshape(cols, slab, size)
    product = nn(band_strip[...], lowered[...])
    send_mats[:, 1] = (product - cross[:, 2 * size :]).reshape(cols, slab, size)
    finish(along_cols, 1, lands.at[1])
    band_all = full(lands[1])

    upper_rows = pl.ds(size, 2 * size)
    for p in range(PASSES):
        first = p == 0
        base = 2 + 8 * p
        pushed = strip_term + nt(band_all, link[...])
        sends[base] = parts(pushed, rows)
        scatter(along_rows, base, sends.at[base], lands.at[base])
        spare = (strip_now * (1.0 / rows) - pushed).astype(BF16)
        if not first:
            summit_term = term(now, keys, 2)
        raised = summit_term + nn(band_all, lift[...]) + nn(spare, lowered[...])
        sends[base + 1] = parts(raised, cols)
        scatter(along_cols, base + 1, sends.at[base + 1], lands.at[base + 1])
        if first:
            scatter(along_cols, extra + 2, send_mats, land_mats.at[0])
            finish(along_cols, extra, land_mat.at[0])
            spread(along_cols, extra + 1, total(land_mat[0]), land_mat.at[1])
        else:
            for i in range(pairs):
                forward_step(i)
        finish(along_rows, base, lands.at[base])
        rest = strip_src - total(lands[base])
        strip_slab = rounded(nt(rest.astype(BF16), sinv[...]))
        spread(along_rows, base + 2, strip_slab, lands.at[base + 2])
        finish(along_cols, base + 1, lands.at[base + 1])
        own = total(lands[base + 1])
        land_twin[p, 0] = own
        meet(base + 3, land_twin.at[p, 0], land_twin.at[p, 1])
        backward_chain()
        if first:
            next_term = term(solved, keys, 0)
        gather(base + 3, land_twin.at[p, 0], land_twin.at[p, 1])
        spread(along_chips, base + 4, own + land_twin[p, 1], lands.at[base + 4])
        finish(along_rows, base + 2, lands.at[base + 2])
        strip_all = full(lands[base + 2])
        dropped = nn(strip_all, joined[...])
        strip_own = nn(strip_all, sinv[...])
        if first:
            send_pair[:, 0] = parts(dropped, cols)
            next_term = next_term - nt(strip_own.astype(BF16), band_strip[...])
            send_pair[:, 1] = parts(next_term, cols)
            scatter(along_cols, base + 5, send_pair, land_pair.at[0])
            finish(along_cols, extra + 2, land_mats.at[0])
            spread(along_cols, extra + 3, total(land_mats[0]), land_mats.at[1])
            finish(along_cols, extra + 1, land_mat.at[1])
            ahead_all[...] = land_mat[1].reshape(size, size).astype(BF16)
        else:
            sends[base + 5] = parts(dropped, cols)
            scatter(along_cols, base + 5, sends.at[base + 5], lands.at[base + 5])
        finish(along_chips, base + 4, lands.at[base + 4])
        rest = summit_src - total(lands[base + 4, : rows // 2])
        top = nt(rest.astype(BF16), uinv[...]).astype(BF16)
        top = nn(top, uinv[...]).astype(BF16)
        summit_src = top.astype(F32)
        spread(along_cols, base + 6, summit_src, lands.at[base + 6])
        back = nt(top, ahead_all[...])
        if first:
            finish(along_cols, base + 5, land_pair.at[0])
            sums = total(land_pair[0])
            rest = band_slab - sums[0] + back
            band_answer = rounded(nn(rest.astype(BF16), binv[...]))
            shift = nt(sums[1].astype(BF16), binv[...])
            spread(along_cols, base + 7, jnp.stack([band_answer, shift]), land_pair.at[1])
        else:
            finish(along_cols, base + 5, lands.at[base + 5])
            rest = band_slab - total(lands[base + 5]) + back
            band_answer = rounded(nn(rest.astype(BF16), binv[...]))
            spread(along_cols, base + 7, band_answer, lands.at[base + 7])
        finish(along_cols, base + 6, lands.at[base + 6])
        top_all = full(lands[base + 6])
        strip_answer = (strip_own - nt(top_all, lowered[...])).astype(BF16)
        strip_now = strip_answer.astype(F32)
        upper = jnp.concatenate([strip_answer, top_all], axis=1)
        for a in range(leaves):
            rest = pend[a] - nn(upper, keys[a, upper_rows, :])
            pend[a] = rest
            if first:
                now[a] = rest.astype(BF16)
        if first:
            slabs[1] = parts(strip_now, rows)
            strip_src = slabs[1, r]
            strip_term = term(now, keys, 1)
            finish(along_cols, extra + 3, land_mats.at[1])
            fold = land_mats[1, :, 0].reshape(size, size).astype(BF16)
            ahead_mat = binv[...].astype(F32) + nn(binv[...], fold)
            ahead_mat = ahead_mat.astype(BF16)
            fold = land_mats[1, :, 1].reshape(size, size).astype(BF16)
            lag = nn(binv[...], fold).astype(BF16)
            lagging = nt(top_all, lag)
            finish(along_cols, base + 7, land_pair.at[1])
            band_full = full(land_pair[1, :, 0])
            lagging = lagging + land_pair[1, :, 1].reshape(count, size)
            band_next = nt(band_full, ahead_mat) - lagging
            band_all = band_next.astype(BF16)
            band_place = rounded(band_next).reshape(cols, count // cols, size)
            slabs[0] = band_place
            band_slab = slabs[0, c]
            strip_term = strip_term - nn(band_full, band_strip[...])
        else:
            finish(along_cols, base + 7, lands.at[base + 7])
            band_full = full(lands[base + 7])
        for a in range(leaves):
            value = (pend[a] - nn(band_full, keys[a, low, :])).astype(BF16)
            if first:
                now[a] = value
            else:
                leaf_out[a] = value
    border_out[0] = band_full
    border_out[1] = strip_answer
    border_out[2] = top_all
    for peers, land, phase in used:
        bytes_of(peers, land, phase).wait_send()


def turn(leaf_in, border_in, leaf_out, band_out, strip_out, summit_out):
    for a in range(leaf_in.shape[0]):
        leaf_out[a] = leaf_in[a].astype(F32).T.astype(BF16)
    for place, out in enumerate((band_out, strip_out, summit_out)):
        out[...] = border_in[place].astype(F32).T.astype(BF16)


def per_device(
    rows,
    cols,
    leaf_source,
    band_source,
    strip_source,
    summit_source,
    leaf_inverse,
    band_inverse,
    strip_inverse,
    summit_inverse,
    leaf_blocks,
    band_blocks,
    strip_blocks,
    summit_blocks,
    coupling,
    summit_band,
    summit_strip,
    parents,
    widths,
):
    leaves, size, count = leaf_source.shape[2:]
    pairs = leaf_blocks.shape[2]
    slab = summit_band.shape[1]
    band_rhs = count // cols
    square = (size, size)
    anywhere = pl.BlockSpec(memory_space=pl.ANY)
    scalars = pl.BlockSpec(memory_space=pltpu.SMEM)
    vmem = pl.BlockSpec(memory_space=pltpu.VMEM)
    plain = pltpu.VMEM(square, BF16)
    phases = 6 + 8 * PASSES
    solved = pl.pallas_call(
        functools.partial(kernel, rows, cols),
        out_shape=(
            jax.ShapeDtypeStruct((leaves, count, size), BF16),
            jax.ShapeDtypeStruct((3, count, size), BF16),
        ),
        in_specs=[scalars] * 2 + [anywhere] * 15,
        out_specs=(vmem,) * 2,
        scratch_shapes=[
            pltpu.VMEM((leaves, size, count), BF16),
            pltpu.VMEM((3, size, count), BF16),
            pltpu.VMEM((leaves,) + square, BF16),
            pltpu.VMEM((pairs,) + square, BF16),
            pltpu.VMEM((leaves // 2,) + square, BF16),
            pltpu.VMEM((leaves, 3 * size, size), BF16),
            pltpu.VMEM((leaves, 3 * size, size), BF16),
            plain,
            plain,
            plain,
            plain,
            pltpu.VMEM((slab, size), BF16),
            plain,
            plain,
            plain,
            plain,
            pltpu.VMEM((leaves, count, size), BF16),
            pltpu.VMEM((leaves, size, count), BF16),
            pltpu.VMEM((leaves, count, size), BF16),
            pltpu.VMEM((leaves, count, size), F32),
            pltpu.VMEM((3, cols, band_rhs, size), F32),
            pltpu.VMEM((phases, cols, band_rhs, size), F32),
            pltpu.VMEM((cols, slab, size), F32),
            pltpu.VMEM((cols, 2, slab, size), F32),
            pltpu.VMEM((cols, 2, band_rhs, size), F32),
            pltpu.VMEM((phases, cols, band_rhs, size), F32),
            pltpu.VMEM((2, cols, slab, size), F32),
            pltpu.VMEM((2, cols, 2, slab, size), F32),
            pltpu.VMEM((2, cols, 2, band_rhs, size), F32),
            pltpu.VMEM((PASSES, 2, band_rhs, size), F32),
            plain,
            plain,
            pltpu.SemaphoreType.DMA((32,)),
            pltpu.SemaphoreType.DMA((phases,)),
            pltpu.SemaphoreType.DMA((phases,)),
        ],
        compiler_params=pltpu.CompilerParams(
            collective_id=0, has_side_effects=True, vmem_limit_bytes=56 * 1024 * 1024
        ),
        cost_estimate=pl.CostEstimate(
            flops=4_400_000_000, bytes_accessed=10_000_000, transcendentals=0
        ),
    )(
        parents[0, 0],
        widths[0, 0],
        leaf_source[0, 0],
        band_source[0],
        strip_source[0],
        summit_source,
        leaf_inverse[0, 0],
        band_inverse[0],
        strip_inverse[0],
        summit_inverse,
        leaf_blocks[0, 0],
        band_blocks[0, 0],
        strip_blocks[0, 0],
        summit_blocks[0, 0],
        coupling[0, 0],
        summit_band[0],
        summit_strip[0],
    )
    results = pl.pallas_call(
        turn,
        out_shape=(
            jax.ShapeDtypeStruct((leaves, size, count), BF16),
            jax.ShapeDtypeStruct((size, count), BF16),
            jax.ShapeDtypeStruct((size, count), BF16),
            jax.ShapeDtypeStruct((size, count), BF16),
        ),
        in_specs=[vmem] * 2,
        out_specs=(vmem,) * 4,
    )(*solved)
    return results[0][None, None], results[1][None], results[2][None], results[3]


def solution(mesh):
    placed = (
        P("prow", "pcol", None, None, None),
        P("prow", None, None),
        P("pcol", None, None),
        P(),
        P("prow", "pcol", None, None, None),
        P("prow", None, None),
        P("pcol", None, None),
        P(),
        P("prow", "pcol", None, None, None),
        P("prow", "pcol", None, None, None),
        P("prow", "pcol", None, None, None),
        P("prow", "pcol", None, None, None),
        P("prow", "pcol", None, None),
        P("prow", "pcol", None),
        P("pcol", None, None),
        P("prow", "pcol", None),
        P("prow", "pcol", None),
    )
    return jax.shard_map(
        functools.partial(per_device, mesh.shape["prow"], mesh.shape["pcol"]),
        mesh=mesh,
        in_specs=placed,
        out_specs=(
            P("prow", "pcol", None, None, None),
            P("prow", None, None),
            P("pcol", None, None),
            P(),
        ),
        check_vma=False,
    )
```
